32 devices in a mesh: rowk: 4 (over z), colk: 8 (over y, x, core).
Axes of the slice: x: 2, y: 2, z: 4, core: 2. Of those that a mesh axis runs over, the one named last changes fastest.
Arguments:
- coarse_kernel: bfloat16 [64, 64, 128, 128], P(('rowk', 'colk')), may hold values from -0.03125 to 0.03125
- left_rotation: bfloat16 [128, 2, 128, 128], P('rowk'), may hold values from -0.5 to 0.5
- right_rotation: bfloat16 [128, 2, 128, 128], P('colk'), may hold values from -0.5 to 0.5
- fine_map: int32 [128], replicated, may hold values from 0 to 63, as said below
- coefficient_index: int32 [128, 128, 4], P('rowk', 'colk'), may hold values from 0 to 15, as said below
- coefficient_table: float32 [16], replicated, may hold values from 0.3 to 1
- trial_vectors: bfloat16 [64, 16384], P(None, 'colk'), may hold values from -6 to 6
Outputs:
- forward_image: bfloat16 [64, 16384], P(None, ('rowk', 'colk'))
- adjoint_image: bfloat16 [64, 16384], P('rowk', 'colk')
The draws below stay inside these ranges and needn't reach their ends.
Inputs may be any that keep to these rules, and one draw needn't show every extreme that they name: `fine_map`: entry i is i // 2 or i // 2 - 1 and lies in the same aligned group of 8 coarse points as i // 2; it equals i // 2 where i // 2 is the first or the last of its group. `coefficient_index`: 0 marks an absent source; slot 0 is never 0.
All inputs are finite; a program needn't handle non-finite values.
Results may differ from the reference program's by a relative error of at most 0.018.
Values may be sent and summed in bfloat16 or wider, within the bound.
A program may use at most 128 MiB of HBM per device.

```python
import jax
import jax.numpy as jnp
from jax import lax

NB = 128
VECS = 64
NCOEF = 16
NKF = 128
NKC = 64
CCOL = 8
NDIM = 16384


def draw_fine_map(key, part):
    halves = jnp.arange(NKF, dtype=jnp.int32) // 2
    steps = jax.random.randint(jax.random.fold_in(key, 11), (NKF,), 0, 2, dtype=jnp.int32)
    position = halves % CCOL
    steps = jnp.where((position == 0) | (position == CCOL - 1), 0, steps)
    return (halves - steps).astype(jnp.int32)


def draw_coefficient_index(key, part):
    base = jax.random.fold_in(key, 23)
    level_rows = jax.random.randint(jax.random.fold_in(base, 1), (NKF,), 0, 4, dtype=jnp.int32)
    level_cols = jax.random.randint(jax.random.fold_in(base, 2), (NKF,), 0, 4, dtype=jnp.int32)
    trials = jax.random.randint(jax.random.fold_in(base, 3), (NKF, NKF, 4), 0, 4, dtype=jnp.int32)
    level = jnp.maximum(level_rows[:, None], level_cols[None, :])
    keeps = trials <= level[:, :, None]
    slots = jnp.arange(4, dtype=jnp.int32)[None, None, :]
    keeps = keeps | (slots == 0)
    values = jax.random.randint(jax.random.fold_in(base, 4), (NKF, NKF, 4), 1, NCOEF, dtype=jnp.int32)
    return jnp.where(keeps, values, 0).astype(jnp.int32)


def block_scale(rng, dims, cuts, smallest, high):
    gain, own = 1.0, jax.random.fold_in(rng, 6)
    for axis_at, shards_of in cuts:
        steps = jnp.exp(jax.random.uniform(jax.random.fold_in(own, axis_at), (shards_of,), jnp.float32, smallest / len(cuts), high / len(cuts)))
        gain = gain * jnp.repeat(steps, dims[axis_at] // shards_of).reshape([-1 if axis == axis_at else 1 for axis in range(len(dims))])
    return gain


def gaussian(key, dims, scale, bound, shards=(), held_as=jnp.bfloat16):
    array = jax.random.normal(key, dims, jnp.float32) * scale
    if len(shards) > 0:
        array = block_scale(key, dims, shards, -0.22, 0.18) * array
    return jnp.clip(array, min=-bound, max=bound).astype(held_as)


def setup_inputs(seed: int = 0) -> dict:
    key_of = jax.random.split(jax.random.key(seed), 8)
    return {
        "coarse_kernel": gaussian(key_of[0], (NKC, NKC, NB, NB), (2 * NKF * NB) ** -0.5, 0.03125, ((0, 32),)),
        "left_rotation": gaussian(key_of[1], (NKF, 2, NB, NB), NB ** -0.5, 0.5, ((0, 4),)),
        "right_rotation": gaussian(key_of[2], (NKF, 2, NB, NB), NB ** -0.5, 0.5, ((0, 8),)),
        "fine_map": draw_fine_map(jax.random.fold_in(key_of[7], 71), 0),
        "coefficient_index": draw_coefficient_index(jax.random.fold_in(key_of[7], 71), 0),
        "coefficient_table": jnp.clip(jax.random.uniform(key_of[5], (NCOEF,), jnp.float32, 0.3, 1.0), 0.3, 1.0),
        "trial_vectors": gaussian(key_of[6], (VECS, NDIM), 1.0, 6.0, ((1, 8),)),
    }


def reference(coarse_kernel, left_rotation, right_rotation, fine_map, coefficient_index, coefficient_table, trial_vectors):
    picked = coefficient_table[coefficient_index]
    weight = jnp.where(coefficient_index > 0, picked, jnp.zeros_like(picked)).astype(jnp.float32)
    offsets = jnp.arange(2, dtype=jnp.int32)
    col_source = ((fine_map[:, None] + offsets[None, :]) % NKC).astype(jnp.int32)

    def tile_row(index):
        row_source = ((fine_map[index] + offsets) % NKC).astype(jnp.int32)
        blocks = coarse_kernel[row_source[:, None, None], col_source[None, :, :]]
        shared = jnp.einsum('pjqab,jqbc->pjqac', blocks.astype(jnp.float32), right_rotation.astype(jnp.float32)).astype(jnp.bfloat16)
        row_weight = weight[index].reshape(NKF, 2, 2).transpose(1, 0, 2)
        mixed = (row_weight[:, :, 0, None, None] * shared[:, :, 0] + row_weight[:, :, 1, None, None] * shared[:, :, 1]).astype(jnp.bfloat16)
        rotor = left_rotation[index].astype(jnp.float32)
        return jnp.einsum('pba,pjbc->jac', rotor, mixed.astype(jnp.float32)).astype(jnp.bfloat16)

    vec_cols = trial_vectors.reshape(VECS, NKF, NB).astype(jnp.float32)

    def forward_row(index):
        tiles = tile_row(index).astype(jnp.float32)
        return jnp.einsum('jac,vjc->va', tiles, vec_cols)

    forward_rows = lax.map(forward_row, jnp.arange(NKF, dtype=jnp.int32))
    forward_image = forward_rows.transpose(1, 0, 2).reshape(VECS, NKF * NB).astype(jnp.bfloat16)
    forward_three = forward_image.reshape(VECS, NKF, NB).astype(jnp.float32)

    def back_step(total, index):
        tiles = tile_row(index).astype(jnp.float32)
        rows_now = forward_three[:, index, :]
        return total + jnp.einsum('jac,va->vjc', tiles, rows_now), None

    start_total = jnp.zeros((VECS, NKF, NB), jnp.float32)
    total, unused = lax.scan(back_step, start_total, jnp.arange(NKF, dtype=jnp.int32))
    adjoint_image = total.reshape(VECS, NKF * NB).astype(jnp.bfloat16)
    return forward_image, adjoint_image
```

```python
import functools

import jax
import jax.numpy as jnp
from jax import lax
from jax.experimental import pallas as pl
from jax.experimental.pallas import tpu as pltpu
from jax.sharding import PartitionSpec as P

MESH = pl.DeviceIdType.MESH
F32 = jnp.float32
BF16 = jnp.bfloat16


def dot_nt(left, right):
    return lax.dot_general(left, right, (((1,), (1,)), ((), ())), preferred_element_type=F32)


def dot_nn(left, right):
    return lax.dot_general(left, right, (((1,), (0,)), ((), ())), preferred_element_type=F32)


def operator_kernel(
    sizes,
    kernel_ref, left_ref, right_ref, row_pick, col_pick, mix_ref, vec_ref,
    forward_ref, adjoint_ref,
    blocks, turned, wide, coarse_image, part_out, part_in, gathered, lifted, wide_back, slot_image,
    back_out, back_in,
    own_sem, main_send, main_recv, rim_send, rim_recv, relay_send, relay_recv,
    part_send, part_recv, row_send, row_recv, back_send, back_recv,
):
    n_rows, n_cols, held, p_count, q_count, fine_rows, fine_cols, nb, vecs, j_pad = sizes
    row_id, col_id = lax.axis_index("rowk"), lax.axis_index("colk")
    coarse_cols = q_count - 1
    chunk = fine_rows // n_cols
    share = vecs // n_rows

    def column_peer(offset):
        return lax.rem(col_id + offset, n_cols)

    def row_peer(offset):
        return lax.rem(row_id + offset, n_rows)

    barrier = pltpu.get_barrier_semaphore()
    for offset in range(1, n_cols):
        pl.semaphore_signal(barrier, inc=1, device_id=(row_id, column_peer(offset)), device_id_type=MESH)
    for offset in range(1, n_rows):
        pl.semaphore_signal(barrier, inc=1, device_id=(row_peer(offset), col_id), device_id_type=MESH)
    pl.semaphore_wait(barrier, n_cols - 1 + n_rows - 1)

    sends = []
    for row in range(held):
        place = col_id * held + row
        for offset in range(1, n_cols):
            peer = column_peer(offset)
            rim = lax.rem(peer + 1, n_cols) * coarse_cols
            at = row * n_cols + offset
            sends.append(pltpu.make_async_remote_copy(
                src_ref=kernel_ref.at[row, pl.ds(peer * coarse_cols, coarse_cols)],
                dst_ref=blocks.at[pl.ds(0, coarse_cols), place],
                send_sem=main_send.at[at], recv_sem=main_recv.at[place],
                device_id=(row_id, peer), device_id_type=MESH,
            ))
            sends.append(pltpu.make_async_remote_copy(
                src_ref=kernel_ref.at[row, rim], dst_ref=blocks.at[coarse_cols, place],
                send_sem=rim_send.at[at], recv_sem=rim_recv.at[place],
                device_id=(row_id, peer), device_id_type=MESH,
            ))
    own = []
    for row in range(held):
        place = col_id * held + row
        rim = lax.rem(col_id + 1, n_cols) * coarse_cols
        own.append(pltpu.make_async_copy(
            kernel_ref.at[row, pl.ds(col_id * coarse_cols, coarse_cols)],
            blocks.at[pl.ds(0, coarse_cols), place], own_sem.at[row, 0],
        ))
        own.append(pltpu.make_async_copy(
            kernel_ref.at[row, rim], blocks.at[coarse_cols, place], own_sem.at[row, 1],
        ))
    for copy in sends + own:
        copy.start()

    turned[...] = jnp.zeros_like(turned)
    lifted[...] = jnp.zeros_like(lifted)

    def turn(j, carry):
        vec = vec_ref[:, pl.ds(pl.multiple_of(j * nb, nb), nb)]
        for slot in range(3):
            side = jnp.clip(col_pick[j] - 1 + slot, 0, 1)
            turned[j + 2, slot] = dot_nt(vec, right_ref[j, side])
        return carry

    lax.fori_loop(0, fine_cols, turn, 0)

    def scale(i, slot, j, other):
        return mix_ref[((i * 3 + slot) * j_pad + j) * 3 + other]

    half = vecs // 2

    def widen(step, carry):
        q, p = step // p_count, step % p_count
        for part in range(2):
            rows = pl.ds(part * half, half)
            tiles = [turned[2 * q + b, 2 - b // 2, rows] for b in range(6)]
            for a in range(6):
                total = scale(2 * p + a, 2 - a // 2, 2 * q, 2) * tiles[0]
                for b in range(1, 6):
                    total += scale(2 * p + a, 2 - a // 2, 2 * q + b, 2 - b // 2) * tiles[b]
                wide[p, pl.ds(a * vecs + part * half, half), pl.ds(pl.multiple_of(q * nb, nb), nb)] = total.astype(BF16)
        return carry

    lax.fori_loop(0, p_count * q_count, widen, 0)

    def contract(p):
        matrix = jnp.concatenate([blocks[q, p] for q in range(q_count)], axis=1)
        coarse_image[p] = dot_nt(wide[p], matrix).astype(BF16)

    relay = pltpu.make_async_remote_copy(
        src_ref=blocks.at[:, 0], dst_ref=blocks.at[:, p_count - 1],
        send_sem=relay_send, recv_sem=relay_recv,
        device_id=(row_peer(n_rows - 1), col_id), device_id_type=MESH,
    )

    def pass_on(place):
        @pl.when(place == 0)
        def _():
            relay.start()

    def take(step, carry):
        row, offset = step // (n_cols - 1), step % (n_cols - 1) + 1
        source = lax.rem(col_id - offset + n_cols, n_cols)
        place = source * held + row
        pltpu.make_async_remote_copy(
            src_ref=blocks.at[pl.ds(0, coarse_cols), place], dst_ref=blocks.at[pl.ds(0, coarse_cols), place],
            send_sem=main_send.at[0], recv_sem=main_recv.at[place],
            device_id=(row_id, source), device_id_type=MESH,
        ).wait_recv()
        pltpu.make_async_remote_copy(
            src_ref=blocks.at[coarse_cols, place], dst_ref=blocks.at[coarse_cols, place],
            send_sem=rim_send.at[0], recv_sem=rim_recv.at[place],
            device_id=(row_id, source), device_id_type=MESH,
        ).wait_recv()
        pass_on(place)
        contract(place)
        return carry

    for copy in own:
        copy.wait()
    pass_on(col_id * held)
    for row in range(held):
        contract(col_id * held + row)
    lax.fori_loop(0, held * (n_cols - 1), take, 0)
    relay.wait_recv()
    contract(p_count - 1)

    def part_of(target):
        for k in range(chunk):
            i = target * chunk + k
            total = None
            for slot in range(3):
                side = jnp.clip(row_pick[i] - 1 + slot, 0, 1)
                place = jnp.maximum(i // 2 - 1 + slot, 0)
                at = (2 - slot) * 2 + i % 2
                image = coarse_image[place, pl.ds(pl.multiple_of(at * vecs, vecs), vecs)]
                term = dot_nn(image, left_ref[i, side])
                usable = jnp.where(i // 2 - 1 + slot >= 0, 1.0, 0.0)
                total = term * usable if total is None else total + term
            part_out[target, :, pl.ds(k * nb, nb)] = total.astype(BF16)

    def part_copy(offset):
        peer = column_peer(offset)
        return pltpu.make_async_remote_copy(
            src_ref=part_out.at[peer], dst_ref=part_in.at[col_id],
            send_sem=part_send.at[offset], recv_sem=part_recv.at[col_id],
            device_id=(row_id, peer), device_id_type=MESH,
        )

    def send_part(offset, carry):
        part_of(column_peer(offset))
        part_copy(offset).start()
        return carry

    lax.fori_loop(1, n_cols, send_part, 0)
    part_of(col_id)

    def add_part(offset, total):
        source = column_peer(offset)
        pltpu.make_async_remote_copy(
            src_ref=part_in.at[source], dst_ref=part_in.at[source],
            send_sem=part_send.at[0], recv_sem=part_recv.at[source],
            device_id=(row_id, source), device_id_type=MESH,
        ).wait_recv()
        return total + part_in[source].astype(F32)

    total = part_out[col_id].astype(F32)
    for offset in range(1, n_cols):
        total = add_part(offset, total)
    image = total.astype(BF16)
    forward_ref[...] = image
    gathered[col_id] = image

    def row_copy(offset):
        return pltpu.make_async_remote_copy(
            src_ref=gathered.at[col_id], dst_ref=gathered.at[col_id],
            send_sem=row_send.at[offset], recv_sem=row_recv.at[col_id],
            device_id=(row_id, column_peer(offset)), device_id_type=MESH,
        )

    for offset in range(1, n_cols):
        row_copy(offset).start()

    def lift(source):
        for k in range(chunk):
            i = source * chunk + k
            piece = gathered[source, :, pl.ds(k * nb, nb)]
            for slot in range(3):
                side = jnp.clip(row_pick[i] - 1 + slot, 0, 1)
                lifted[i + 2, slot] = dot_nt(piece, left_ref[i, side])

    lift(col_id)

    def lift_next(offset, carry):
        source = lax.rem(col_id - offset + n_cols, n_cols)
        pltpu.make_async_remote_copy(
            src_ref=gathered.at[source], dst_ref=gathered.at[source],
            send_sem=row_send.at[0], recv_sem=row_recv.at[source],
            device_id=(row_id, source), device_id_type=MESH,
        ).wait_recv()
        lift(source)
        return carry

    lax.fori_loop(1, n_cols, lift_next, 0)

    def back(q, carry):
        def mix(p, inner):
            for part in range(2):
                rows = pl.ds(part * half, half)
                tiles = [lifted[2 * p + a, 2 - a // 2, rows] for a in range(6)]
                for b in range(6):
                    total = scale(2 * p, 2, 2 * q + b, 2 - b // 2) * tiles[0]
                    for a in range(1, 6):
                        total += scale(2 * p + a, 2 - a // 2, 2 * q + b, 2 - b // 2) * tiles[a]
                    wide_back[pl.ds(b * vecs + part * half, half), pl.ds(pl.multiple_of(p * nb, nb), nb)] = total.astype(BF16)
            return inner

        lax.fori_loop(0, p_count, mix, 0)
        matrix = jnp.concatenate([blocks[q, p] for p in range(p_count)], axis=0)
        slot_image[q] = dot_nn(wide_back[...], matrix).astype(BF16)
        return carry

    lax.fori_loop(0, q_count, back, 0)

    def finish(j, carry):
        total = None
        for slot in range(3):
            side = jnp.clip(col_pick[j] - 1 + slot, 0, 1)
            place = jnp.maximum(j // 2 - 1 + slot, 0)
            at = (2 - slot) * 2 + j % 2
            image = slot_image[place, pl.ds(pl.multiple_of(at * vecs, vecs), vecs)]
            term = dot_nn(image, right_ref[j, side])
            usable = jnp.where(j // 2 - 1 + slot >= 0, 1.0, 0.0)
            total = term * usable if total is None else total + term
        for target in range(n_rows):
            back_out[target, :, pl.ds(pl.multiple_of(j * nb, nb), nb)] = (
                total[target * share:(target + 1) * share].astype(BF16)
            )
        return carry

    lax.fori_loop(0, fine_cols, finish, 0)

    def back_copy(offset):
        peer = row_peer(offset)
        return pltpu.make_async_remote_copy(
            src_ref=back_out.at[peer], dst_ref=back_in.at[row_id],
            send_sem=back_send.at[offset], recv_sem=back_recv.at[row_id],
            device_id=(peer, col_id), device_id_type=MESH,
        )

    for offset in range(1, n_rows):
        back_copy(offset).start()
    total = back_out[row_id].astype(F32)
    for offset in range(1, n_rows):
        source = row_peer(offset)
        pltpu.make_async_remote_copy(
            src_ref=back_in.at[source], dst_ref=back_in.at[source],
            send_sem=back_send.at[0], recv_sem=back_recv.at[source],
            device_id=(source, col_id), device_id_type=MESH,
        ).wait_recv()
        total = total + back_in[source].astype(F32)
    adjoint_ref[...] = total.astype(BF16)

    for copy in sends:
        copy.wait_send()
    relay.wait_send()
    for offset in range(1, n_cols):
        part_copy(offset).wait_send()
        row_copy(offset).wait_send()
    for offset in range(1, n_rows):
        back_copy(offset).wait_send()


def body(
    coarse_kernel,
    left_rotation,
    right_rotation,
    fine_map,
    coefficient_index,
    coefficient_table,
    trial_vectors,
):
    n_rows = lax.axis_size("rowk")
    n_cols = lax.axis_size("colk")
    row_id = lax.axis_index("rowk")
    col_id = lax.axis_index("colk")
    held, coarse_total = coarse_kernel.shape[:2]
    fine_rows = left_rotation.shape[0]
    fine_cols = right_rotation.shape[0]
    nb = left_rotation.shape[2]
    vecs = trial_vectors.shape[0]
    p_count = coarse_total // n_rows + 1
    q_count = coarse_total // n_cols + 1
    chunk = fine_rows // n_cols
    share = vecs // n_rows

    pick = jnp.arange(fine_map.shape[0], dtype=jnp.int32) // 2 - fine_map
    row_pick = lax.dynamic_slice_in_dim(pick, row_id * fine_rows, fine_rows)
    col_pick = lax.dynamic_slice_in_dim(pick, col_id * fine_cols, fine_cols)

    entries = jnp.arange(coefficient_table.shape[0], dtype=jnp.int32)
    match = (coefficient_index[..., None] == entries) & (coefficient_index[..., None] > 0)
    weight = jnp.sum(jnp.where(match, coefficient_table, 0.0), axis=-1)
    slots = jnp.arange(3, dtype=jnp.int32)
    row_side = row_pick[:, None] - 1 + slots
    col_side = col_pick[:, None] - 1 + slots
    mix = jnp.zeros((fine_rows, 3, fine_cols, 3), F32)
    for dp in range(2):
        for dq in range(2):
            here = (row_side == dp)[:, :, None, None] & (col_side == dq)[None, None, :, :]
            mix = mix + jnp.where(here, weight[:, None, :, None, 2 * dp + dq], 0.0)
    mix = jnp.pad(mix, ((2, 4), (0, 0), (2, 4), (0, 0)))
    i_pad, j_pad = fine_rows + 6, fine_cols + 6

    sizes = (n_rows, n_cols, held, p_count, q_count, fine_rows, fine_cols, nb, vecs, j_pad)
    vmem = pl.BlockSpec(memory_space=pltpu.VMEM)
    smem = pl.BlockSpec(memory_space=pltpu.SMEM)
    dma = pltpu.SemaphoreType.DMA
    return pl.pallas_call(
        functools.partial(operator_kernel, sizes),
        out_shape=(
            jax.ShapeDtypeStruct((vecs, chunk * nb), BF16),
            jax.ShapeDtypeStruct((share, fine_cols * nb), BF16),
        ),
        in_specs=[pl.BlockSpec(memory_space=pl.ANY), vmem, vmem, smem, smem, smem, vmem],
        out_specs=(vmem, vmem),
        scratch_shapes=[
            pltpu.VMEM((q_count, p_count, nb, nb), BF16),
            pltpu.VMEM((j_pad, 3, vecs, nb), F32),
            pltpu.VMEM((p_count, 6 * vecs, q_count * nb), BF16),
            pltpu.VMEM((p_count, 6 * vecs, nb), BF16),
            pltpu.VMEM((n_cols, vecs, chunk * nb), BF16),
            pltpu.VMEM((n_cols, vecs, chunk * nb), BF16),
            pltpu.VMEM((n_cols, vecs, chunk * nb), BF16),
            pltpu.VMEM((i_pad, 3, vecs, nb), F32),
            pltpu.VMEM((6 * vecs, p_count * nb), BF16),
            pltpu.VMEM((q_count, 6 * vecs, nb), BF16),
            pltpu.VMEM((n_rows, share, fine_cols * nb), BF16),
            pltpu.VMEM((n_rows, share, fine_cols * nb), BF16),
            dma((held, 2)),
            dma((held * n_cols,)),
            dma((held * n_cols,)),
            dma((held * n_cols,)),
            dma((held * n_cols,)),
            dma(()),
            dma(()),
            dma((n_cols,)),
            dma((n_cols,)),
            dma((n_cols,)),
            dma((n_cols,)),
            dma((n_rows,)),
            dma((n_rows,)),
        ],
        compiler_params=pltpu.CompilerParams(
            collective_id=0, has_side_effects=True, vmem_limit_bytes=52 * 1024 * 1024
        ),
        name="operator_images",
    )(
        coarse_kernel, left_rotation, right_rotation, row_pick, col_pick, mix.reshape(-1), trial_vectors
    )


def solution(mesh):
    return jax.shard_map(
        body,
        mesh=mesh,
        in_specs=(
            P(("rowk", "colk"), None, None, None),
            P("rowk", None, None, None),
            P("colk", None, None, None),
            P(),
            P("rowk", "colk", None),
            P(),
            P(None, "colk"),
        ),
        out_specs=(P(None, ("rowk", "colk")), P("rowk", "colk")),
        check_vma=False,
    )
```

```python
import functools

import jax
import jax.numpy as jnp
from jax import lax
from jax.experimental import pallas as pl
from jax.experimental.pallas import tpu as pltpu
from jax.sharding import PartitionSpec as P

MESH = pl.DeviceIdType.MESH
F32 = jnp.float32
BF16 = jnp.bfloat16


def dot_nt(left, right):
    return lax.dot_general(left, right, (((1,), (1,)), ((), ())), preferred_element_type=F32)


def dot_nn(left, right):
    return lax.dot_general(left, right, (((1,), (0,)), ((), ())), preferred_element_type=F32)


def flip(index, bits):
    out, place = index, 1
    while place <= bits:
        if bits & place:
            out = out + place * (1 - 2 * (index // place % 2))
        place *= 2
    return out


def operator_kernel(
    sizes,
    kernel_ref, left_ref, right_ref, map_ref, index_ref, table_ref, vec_ref,
    forward_ref, adjoint_ref,
    blocks, turned, wide, partial, part_out, part_in, gathered, lifted, slots,
    back_out, back_in, mix,
    own_sem, main_send, main_recv, rim_send, rim_recv, near_send, relay_send, relay_recv,
    part_send, part_recv, row_send, row_recv, back_send, back_recv,
):
    n_rows, n_cols, held, p_count, q_count, fine_rows, fine_cols, nb, vecs = sizes
    row_id, col_id = lax.axis_index("rowk"), lax.axis_index("colk")
    coarse_cols = q_count - 1
    chunk = fine_rows // n_cols
    share = vecs // n_rows
    j_pad = fine_cols + 6
    core = col_id % 2
    sibling = flip(col_id, 1)

    far = list(range(2, n_cols))
    orders = ([1] + far, [1] + far[2:4] + far[:2] + far[4:])

    def column_peer(step):
        first, second = orders[0][step], orders[1][step]
        return (1 - core) * flip(col_id, first) + core * flip(col_id, second)

    def row_peer(offset):
        return lax.rem(row_id + offset, n_rows)

    barrier = pltpu.get_barrier_semaphore()
    for offset in range(1, n_cols):
        pl.semaphore_signal(barrier, inc=1, device_id=(row_id, flip(col_id, offset)), device_id_type=MESH)
    for offset in range(1, n_rows):
        pl.semaphore_signal(barrier, inc=1, device_id=(row_peer(offset), col_id), device_id_type=MESH)
    pl.semaphore_wait(barrier, n_cols - 1 + n_rows - 1)

    sends = []
    rims = []
    for row in range(held):
        place = col_id * held + row
        for step in range(n_cols - 1):
            peer = column_peer(step)
            rim = lax.rem(peer + 1, n_cols) * coarse_cols
            at = row * n_cols + step
            main = pltpu.make_async_remote_copy(
                src_ref=kernel_ref.at[row, pl.ds(peer * coarse_cols, coarse_cols)],
                dst_ref=blocks.at[pl.ds(0, coarse_cols), place],
                send_sem=main_send.at[at], recv_sem=main_recv.at[place],
                device_id=(row_id, peer), device_id_type=MESH,
            )
            edge = pltpu.make_async_remote_copy(
                src_ref=kernel_ref.at[row, rim], dst_ref=blocks.at[coarse_cols, place],
                send_sem=rim_send.at[at], recv_sem=rim_recv.at[place],
                device_id=(row_id, peer), device_id_type=MESH,
            )
            sends.append(main)
            main.start()
            rims.append((peer % 2 == 1, edge))
            pl.when(peer % 2 == 1)(edge.start)
    own = []
    for row in range(held):
        place = col_id * held + row
        rim = lax.rem(col_id + 1, n_cols) * coarse_cols
        own.append(pltpu.make_async_copy(
            kernel_ref.at[row, pl.ds(col_id * coarse_cols, coarse_cols)],
            blocks.at[pl.ds(0, coarse_cols), place], own_sem.at[row, 0],
        ))
        own.append(pltpu.make_async_copy(
            kernel_ref.at[row, rim], blocks.at[coarse_cols, place], own_sem.at[row, 1],
        ))
    for copy in own:
        copy.start()

    def row_base(i):
        base = map_ref[row_id * fine_rows + i] - row_id * (p_count - 1)
        return jnp.clip(base, jnp.maximum(i // 2 - 1, 0), i // 2)

    def col_base(j):
        base = map_ref[col_id * fine_cols + j] - col_id * coarse_cols
        return jnp.clip(base, jnp.maximum(j // 2 - 1, 0), j // 2)

    def mix_at(i, dp, j, slot):
        return ((i * 2 + dp) * j_pad + j) * 3 + slot

    def weigh(i, carry):
        for dp in range(2):
            for j in (0, 1, fine_cols + 2, fine_cols + 3, fine_cols + 4, fine_cols + 5):
                for slot in range(3):
                    mix[mix_at(i, dp, j, slot)] = jnp.float32(0.0)

        def one(j, inner):
            lower = col_base(j) < j // 2
            for dp in range(2):
                pair = []
                for dq in range(2):
                    entry = index_ref[(i * fine_cols + j) * 4 + 2 * dp + dq]
                    pair.append(jnp.where(entry > 0, table_ref[entry], 0.0))
                mix[mix_at(i, dp, j + 2, 0)] = jnp.where(lower, pair[0], 0.0)
                mix[mix_at(i, dp, j + 2, 1)] = jnp.where(lower, pair[1], pair[0])
                mix[mix_at(i, dp, j + 2, 2)] = jnp.where(lower, 0.0, pair[1])
            return inner

        return lax.fori_loop(0, fine_cols, one, carry)

    lax.fori_loop(0, fine_rows, weigh, 0)

    turned[...] = jnp.zeros_like(turned)
    partial[...] = jnp.zeros_like(partial)

    def turn(j, carry):
        vec = vec_ref[:, pl.ds(pl.multiple_of(j * nb, nb), nb)]
        for slot in range(3):
            side = jnp.clip(j // 2 - 1 + slot - col_base(j), 0, 1)
            turned[j + 2, slot] = dot_nt(vec, right_ref[j, side])
        return carry

    lax.fori_loop(0, fine_cols, turn, 0)

    half = vecs // 2

    def widen(step, carry):
        q, pair = step // (fine_rows // 2), step % (fine_rows // 2)
        for part in range(2):
            rows = pl.ds(part * half, half)
            tiles = [turned[2 * q + b, 2 - b // 2, rows] for b in range(6)]
            for k in range(2):
                for dp in range(2):
                    i = 2 * pair + k
                    total = mix[mix_at(i, dp, 2 * q, 2)] * tiles[0]
                    for b in range(1, 6):
                        total += mix[mix_at(i, dp, 2 * q + b, 2 - b // 2)] * tiles[b]
                    wide[i, dp, q, rows] = total.astype(BF16)
        return carry

    lax.fori_loop(0, q_count * (fine_rows // 2), widen, 0)

    def around(p, a):
        i = jnp.clip(2 * p - 2 + a, 0, fine_rows - 1)
        return i, p - row_base(i)

    def contract(p):
        bands = []
        for a in range(6):
            i, dp = around(p, a)
            side = jnp.clip(dp, 0, 1)
            bands.append(jnp.concatenate([wide[i, side, q] for q in range(q_count)], axis=1))
        matrix = jnp.concatenate([blocks[q, p] for q in range(q_count)], axis=1)
        image = dot_nt(jnp.concatenate(bands, axis=0), matrix).astype(BF16)
        for a in range(6):
            i, dp = around(p, a)
            inside = (2 * p - 2 + a == i) & (dp >= 0) & (dp <= 1)
            term = dot_nn(image[a * vecs:(a + 1) * vecs], left_ref[i, jnp.clip(dp, 0, 1)])
            partial[i] += term * jnp.where(inside, 1.0, 0.0)

    relay = pltpu.make_async_remote_copy(
        src_ref=blocks.at[:, 0], dst_ref=blocks.at[:, p_count - 1],
        send_sem=relay_send, recv_sem=relay_recv,
        device_id=(row_peer(n_rows - 1), col_id), device_id_type=MESH,
    )

    def near_copy(place):
        return pltpu.make_async_remote_copy(
            src_ref=blocks.at[0, place], dst_ref=blocks.at[coarse_cols, place],
            send_sem=near_send.at[place], recv_sem=rim_recv.at[place],
            device_id=(row_id, sibling), device_id_type=MESH,
        )

    def wait_rim(place):
        pltpu.make_async_remote_copy(
            src_ref=blocks.at[coarse_cols, place], dst_ref=blocks.at[coarse_cols, place],
            send_sem=rim_send.at[0], recv_sem=rim_recv.at[place],
            device_id=(row_id, sibling), device_id_type=MESH,
        ).wait_recv()

    def use(place):
        @pl.when(place == 0)
        def _():
            relay.start()

        contract(place)

    def take(row, offset):
        source = lax.rem(col_id // 2 + offset // 2, n_cols // 2) * 2 + lax.rem(core + offset, 2)
        place = source * held + row
        pltpu.make_async_remote_copy(
            src_ref=blocks.at[pl.ds(0, coarse_cols), place], dst_ref=blocks.at[pl.ds(0, coarse_cols), place],
            send_sem=main_send.at[0], recv_sem=main_recv.at[place],
            device_id=(row_id, source), device_id_type=MESH,
        ).wait_recv()

        @pl.when((core == 1) & (offset != 1))
        def _():
            near_copy(place).start()

        wait_rim(place)
        use(place)

    for copy in own:
        copy.wait()
    @pl.when(core == 1)
    def _():
        for row in range(held):
            near_copy(col_id * held + row).start()

    for row in range(held):
        use(col_id * held + row)

    def take_step(step, carry):
        take(step // (n_cols - 1), step % (n_cols - 1) + 1)
        return carry

    lax.fori_loop(0, held * (n_cols - 1), take_step, 0)
    relay.wait_recv()
    contract(p_count - 1)

    def part_copy(step):
        peer = column_peer(step)
        return pltpu.make_async_remote_copy(
            src_ref=part_out.at[peer], dst_ref=part_in.at[col_id],
            send_sem=part_send.at[step], recv_sem=part_recv.at[col_id],
            device_id=(row_id, peer), device_id_type=MESH,
        )

    def fill_part(target):
        for k in range(chunk):
            part_out[target, :, pl.ds(k * nb, nb)] = partial[target * chunk + k].astype(BF16)

    backwards = list(range(n_cols - 2, -1, -1))
    for step in backwards:
        fill_part(column_peer(step))
        part_copy(step).start()
    fill_part(col_id)

    total = part_out[col_id].astype(F32)
    for offset in range(1, n_cols):
        source = flip(col_id, offset)
        pltpu.make_async_remote_copy(
            src_ref=part_in.at[source], dst_ref=part_in.at[source],
            send_sem=part_send.at[0], recv_sem=part_recv.at[source],
            device_id=(row_id, source), device_id_type=MESH,
        ).wait_recv()
        total = total + part_in[source].astype(F32)
    image = total.astype(BF16)
    gathered[col_id] = image

    def row_copy(step):
        return pltpu.make_async_remote_copy(
            src_ref=gathered.at[col_id], dst_ref=gathered.at[col_id],
            send_sem=row_send.at[step], recv_sem=row_recv.at[col_id],
            device_id=(row_id, column_peer(step)), device_id_type=MESH,
        )

    for step in backwards:
        row_copy(step).start()
    forward_ref[...] = image

    def lift(source):
        for k in range(chunk):
            i = source * chunk + k
            piece = gathered[source, :, pl.ds(k * nb, nb)]
            both = dot_nt(piece, left_ref[i].reshape(2 * nb, nb)).astype(BF16)
            lifted[i, 0] = both[:, :nb]
            lifted[i, 1] = both[:, nb:]

    lift(col_id)

    def lift_next(step, carry):
        offset = step + 1
        source = lax.rem(col_id // 2 + offset // 2, n_cols // 2) * 2 + lax.rem(core + offset, 2)
        pltpu.make_async_remote_copy(
            src_ref=gathered.at[source], dst_ref=gathered.at[source],
            send_sem=row_send.at[0], recv_sem=row_recv.at[source],
            device_id=(row_id, source), device_id_type=MESH,
        ).wait_recv()
        lift(source)
        return carry

    lax.fori_loop(0, n_cols - 1, lift_next, 0)

    def spread(p, carry):
        bands = []
        for a in range(6):
            i, dp = around(p, a)
            bands.append(lifted[i, jnp.clip(dp, 0, 1)])
        matrix = jnp.concatenate([blocks[q, p] for q in range(q_count)], axis=1)
        image = dot_nn(jnp.concatenate(bands, axis=0), matrix).astype(BF16)
        for q in range(q_count):
            for a in range(6):
                slots[p, q, a] = image[a * vecs:(a + 1) * vecs, q * nb:(q + 1) * nb]
        return carry

    lax.fori_loop(0, p_count, spread, 0)

    def back_copy(piece, offset):
        peer = row_peer(offset)
        return pltpu.make_async_remote_copy(
            src_ref=back_out.at[piece, peer], dst_ref=back_in.at[piece, row_id],
            send_sem=back_send.at[piece, offset], recv_sem=back_recv.at[piece, row_id],
            device_id=(peer, col_id), device_id_type=MESH,
        )

    pieces = back_out.shape[0]
    span = fine_cols // pieces
    group = 8
    for piece in range(pieces):
        def finish(step, carry):
            j = piece * span + step
            q = col_base(j)
            slot = 1 + q - j // 2

            def add(block, totals):
                first, second = totals
                for k in range(group):
                    i = block * group + k
                    base = row_base(i)
                    for dp in range(2):
                        p = base + dp
                        a = i - 2 * p + 2
                        at = mix_at(i, dp, j + 2, slot)
                        first = first + mix[at] * slots[p, q, a].astype(F32)
                        second = second + mix[at + 1] * slots[p, q + 1, a].astype(F32)
                return first, second

            zero = jnp.zeros((vecs, nb), F32)
            first, second = lax.fori_loop(0, fine_rows // group, add, (zero, zero))
            both = jnp.concatenate([first.astype(BF16), second.astype(BF16)], axis=1)
            image = dot_nn(both, right_ref[j].reshape(2 * nb, nb))
            for target in range(n_rows):
                back_out[piece, target, :, pl.ds(pl.multiple_of(step * nb, nb), nb)] = (
                    image[target * share:(target + 1) * share].astype(BF16)
                )
            return carry

        lax.fori_loop(0, span, finish, 0)
        for offset in range(1, n_rows):
            back_copy(piece, offset).start()

    for piece in range(pieces):
        total = back_out[piece, row_id].astype(F32)
        for offset in range(1, n_rows):
            source = row_peer(offset)
            pltpu.make_async_remote_copy(
                src_ref=back_in.at[piece, source], dst_ref=back_in.at[piece, source],
                send_sem=back_send.at[piece, 0], recv_sem=back_recv.at[piece, source],
                device_id=(source, col_id), device_id_type=MESH,
            ).wait_recv()
            total = total + back_in[piece, source].astype(F32)
        adjoint_ref[:, pl.ds(piece * span * nb, span * nb)] = total.astype(BF16)

    for copy in sends:
        copy.wait_send()
    for used, copy in rims:
        pl.when(used)(copy.wait_send)

    @pl.when(core == 1)
    def _():
        def settle(step, carry):
            row, offset = step // (n_cols - 1), step % (n_cols - 1)
            offset = offset + jnp.minimum(offset, 1)
            source = lax.rem(col_id // 2 + offset // 2, n_cols // 2) * 2 + lax.rem(core + offset, 2)
            near_copy(source * held + row).wait_send()
            return carry

        lax.fori_loop(0, held * (n_cols - 1), settle, 0)

    relay.wait_send()
    for step in range(n_cols - 1):
        part_copy(step).wait_send()
        row_copy(step).wait_send()
    for piece in range(pieces):
        for offset in range(1, n_rows):
            back_copy(piece, offset).wait_send()


def body(
    coarse_kernel,
    left_rotation,
    right_rotation,
    fine_map,
    coefficient_index,
    coefficient_table,
    trial_vectors,
):
    n_rows = lax.axis_size("rowk")
    n_cols = lax.axis_size("colk")
    held, coarse_total = coarse_kernel.shape[:2]
    fine_rows = left_rotation.shape[0]
    fine_cols = right_rotation.shape[0]
    nb = left_rotation.shape[2]
    vecs = trial_vectors.shape[0]
    p_count = coarse_total // n_rows + 1
    q_count = coarse_total // n_cols + 1
    chunk = fine_rows // n_cols
    share = vecs // n_rows
    pieces = 2

    sizes = (n_rows, n_cols, held, p_count, q_count, fine_rows, fine_cols, nb, vecs)
    vmem = pl.BlockSpec(memory_space=pltpu.VMEM)
    smem = pl.BlockSpec(memory_space=pltpu.SMEM)
    dma = pltpu.SemaphoreType.DMA
    return pl.pallas_call(
        functools.partial(operator_kernel, sizes),
        out_shape=(
            jax.ShapeDtypeStruct((vecs, chunk * nb), BF16),
            jax.ShapeDtypeStruct((share, fine_cols * nb), BF16),
        ),
        in_specs=[pl.BlockSpec(memory_space=pl.ANY), vmem, vmem, smem, smem, smem, vmem],
        out_specs=(vmem, vmem),
        scratch_shapes=[
            pltpu.VMEM((q_count, p_count, nb, nb), BF16),
            pltpu.VMEM((fine_cols + 6, 3, vecs, nb), F32),
            pltpu.VMEM((fine_rows, 2, q_count, vecs, nb), BF16),
            pltpu.VMEM((fine_rows, vecs, nb), F32),
            pltpu.VMEM((n_cols, vecs, chunk * nb), BF16),
            pltpu.VMEM((n_cols, vecs, chunk * nb), BF16),
            pltpu.VMEM((n_cols, vecs, chunk * nb), BF16),
            pltpu.VMEM((fine_rows, 2, vecs, nb), BF16),
            pltpu.VMEM((p_count, q_count, 6, vecs, nb), BF16),
            pltpu.VMEM((pieces, n_rows, share, fine_cols * nb // pieces), BF16),
            pltpu.VMEM((pieces, n_rows, share, fine_cols * nb // pieces), BF16),
            pltpu.SMEM((fine_rows * 2 * (fine_cols + 6) * 3,), F32),
            dma((held, 2)),
            dma((held * n_cols,)),
            dma((p_count,)),
            dma((held * n_cols,)),
            dma((p_count,)),
            dma((p_count,)),
            dma(()),
            dma(()),
            dma((n_cols,)),
            dma((n_cols,)),
            dma((n_cols,)),
            dma((n_cols,)),
            dma((pieces, n_rows)),
            dma((pieces, n_rows)),
        ],
        compiler_params=pltpu.CompilerParams(
            collective_id=0, has_side_effects=True, vmem_limit_bytes=52 * 1024 * 1024
        ),
        name="operator_images",
    )(
        coarse_kernel, left_rotation, right_rotation, fine_map, coefficient_index.reshape(-1),
        coefficient_table, trial_vectors
    )


def solution(mesh):
    return jax.shard_map(
        body,
        mesh=mesh,
        in_specs=(
            P(("rowk", "colk"), None, None, None),
            P("rowk", None, None, None),
            P("colk", None, None, None),
            P(),
            P("rowk", "colk", None),
            P(),
            P(None, "colk"),
        ),
        out_specs=(P(None, ("rowk", "colk")), P("rowk", "colk")),
        check_vma=False,
    )
```

```python
import functools

import jax
import jax.numpy as jnp
from jax import lax
from jax.experimental import pallas as pl
from jax.experimental.pallas import tpu as pltpu
from jax.sharding import PartitionSpec as P

MESH = pl.DeviceIdType.MESH
F32 = jnp.float32
BF16 = jnp.bfloat16


def dot_nt(left, right):
    return lax.dot_general(left, right, (((1,), (1,)), ((), ())), preferred_element_type=F32)


def dot_nn(left, right):
    return lax.dot_general(left, right, (((1,), (0,)), ((), ())), preferred_element_type=F32)


def flip(index, bits):
    out, place = index, 1
    while place <= bits:
        if bits & place:
            out = out + place * (1 - 2 * (index // place % 2))
        place *= 2
    return out


def operator_kernel(
    sizes,
    kernel_ref, left_far, right_far, map_ref, index_ref, table_ref, vec_far,
    forward_ref, adjoint_ref,
    blocks, turned, wide, partial, part_out, part_in, gathered, lifted, slots,
    back_out, back_in, left_ref, right_ref, vec_ref, mix_rows, mix, spot,
    own_sem, load_sem, mix_sem, main_send, main_recv, rim_send, rim_recv, near_send, relay_send, relay_recv,
    part_send, part_recv, row_send, row_recv, back_send, back_recv,
):
    n_rows, n_cols, held, p_count, q_count, fine_rows, fine_cols, nb, vecs = sizes
    row_id, col_id = lax.axis_index("rowk"), lax.axis_index("colk")
    coarse_cols = q_count - 1
    chunk = fine_rows // n_cols
    share = vecs // n_rows
    j_pad = fine_cols + 6
    core = col_id % 2
    sibling = flip(col_id, 1)

    far = list(range(2, n_cols))
    orders = ([1] + far, [1] + far[2:4] + far[:2] + far[4:])

    def column_peer(step):
        first, second = orders[0][step], orders[1][step]
        return (1 - core) * flip(col_id, first) + core * flip(col_id, second)

    def row_peer(offset):
        return lax.rem(row_id + offset, n_rows)

    barrier = pltpu.get_barrier_semaphore()
    for offset in range(1, n_cols):
        pl.semaphore_signal(barrier, inc=1, device_id=(row_id, flip(col_id, offset)), device_id_type=MESH)
    for offset in range(1, n_rows):
        pl.semaphore_signal(barrier, inc=1, device_id=(row_peer(offset), col_id), device_id_type=MESH)
    pl.semaphore_wait(barrier, n_cols - 1 + n_rows - 1)

    sends = []
    rims = []
    for row in range(held):
        place = col_id * held + row
        for step in range(n_cols - 1):
            peer = column_peer(step)
            rim = lax.rem(peer + 1, n_cols) * coarse_cols
            at = row * n_cols + step
            main = pltpu.make_async_remote_copy(
                src_ref=kernel_ref.at[row, pl.ds(peer * coarse_cols, coarse_cols)],
                dst_ref=blocks.at[pl.ds(0, coarse_cols), place],
                send_sem=main_send.at[at], recv_sem=main_recv.at[place],
                device_id=(row_id, peer), device_id_type=MESH,
            )
            edge = pltpu.make_async_remote_copy(
                src_ref=kernel_ref.at[row, rim], dst_ref=blocks.at[coarse_cols, place],
                send_sem=rim_send.at[at], recv_sem=rim_recv.at[place],
                device_id=(row_id, peer), device_id_type=MESH,
            )
            sends.append(main)
            main.start()
            rims.append((peer % 2 == 1, edge))
            pl.when(peer % 2 == 1)(edge.start)
    own = []
    for row in range(held):
        place = col_id * held + row
        rim = lax.rem(col_id + 1, n_cols) * coarse_cols
        own.append(pltpu.make_async_copy(
            kernel_ref.at[row, pl.ds(col_id * coarse_cols, coarse_cols)],
            blocks.at[pl.ds(0, coarse_cols), place], own_sem.at[row, 0],
        ))
        own.append(pltpu.make_async_copy(
            kernel_ref.at[row, rim], blocks.at[coarse_cols, place], own_sem.at[row, 1],
        ))
    for copy in own:
        copy.start()
    loads = [
        pltpu.make_async_copy(far_ref, near_ref, load_sem.at[at])
        for at, (far_ref, near_ref) in enumerate(((vec_far, vec_ref), (right_far, right_ref), (left_far, left_ref)))
    ]
    for copy in loads:
        copy.start()

    def row_base(i):
        base = map_ref[row_id * fine_rows + i] - row_id * (p_count - 1)
        return jnp.clip(base, jnp.maximum(i // 2 - 1, 0), i // 2)

    def col_base(j):
        base = map_ref[col_id * fine_cols + j] - col_id * coarse_cols
        return jnp.clip(base, jnp.maximum(j // 2 - 1, 0), j // 2)

    mix_rows[...] = jnp.zeros_like(mix_rows)

    def weigh(j, carry):
        entry = index_ref[j]
        weight = jnp.zeros(entry.shape, F32)
        for k in range(1, table_ref.shape[0]):
            weight = jnp.where(entry == k, table_ref[k], weight)
        lower = jnp.where(col_base(j) < j // 2, 1.0, 0.0)
        for dp in range(2):
            near, next_one = weight[2 * dp:2 * dp + 1], weight[2 * dp + 1:2 * dp + 2]
            values = (lower * near, lower * next_one + (1.0 - lower) * near, (1.0 - lower) * next_one)
            for slot in range(3):
                mix_rows[pl.ds((j + 2) * 8 + dp * 3 + slot, 1), pl.ds(0, fine_rows)] = values[slot]
        return carry

    lax.fori_loop(0, fine_cols, weigh, 0)
    mix_copy = pltpu.make_async_copy(mix_rows, mix, mix_sem)
    mix_copy.start()

    def locate(i, carry):
        spot[i] = 4 * row_base(i) + i + 8
        return carry

    lax.fori_loop(0, fine_rows, locate, 0)

    turned[...] = jnp.zeros_like(turned)
    partial[...] = jnp.zeros_like(partial)

    def turn(j, carry):
        vec = vec_ref[:, pl.ds(pl.multiple_of(j * nb, nb), nb)]
        for slot in range(3):
            side = jnp.clip(j // 2 - 1 + slot - col_base(j), 0, 1)
            turned[j + 2, slot] = dot_nt(vec, right_ref[j, side])
        return carry

    for copy in loads:
        copy.wait()
    lax.fori_loop(0, fine_cols, turn, 0)
    mix_copy.wait()

    half = vecs // 2

    def widen(q, pair, count):
        for part in range(2):
            rows = pl.ds(part * half, half)
            tiles = [turned[2 * q + b, 2 - b // 2, rows] for b in range(count)]
            for k in range(2):
                for dp in range(2):
                    i = 2 * pair + k
                    total = mix[2 * q * 8 + dp * 3 + 2, i] * tiles[0]
                    for b in range(1, count):
                        total += mix[(2 * q + b) * 8 + dp * 3 + 2 - b // 2, i] * tiles[b]
                    wide[i, dp, q, rows] = total.astype(BF16)

    pairs = fine_rows // 2

    def widen_step(step, carry):
        widen(step // pairs, step % pairs, 6)
        return carry

    def widen_last(pair, carry):
        widen(coarse_cols, pair, 2)
        return carry

    lax.fori_loop(0, coarse_cols * pairs, widen_step, 0)
    lax.fori_loop(0, pairs, widen_last, 0)

    def around(p, a):
        i = jnp.clip(2 * p - 2 + a, 0, fine_rows - 1)
        return i, p - row_base(i)

    def contract(p):
        bands = []
        for a in range(6):
            i, dp = around(p, a)
            side = jnp.clip(dp, 0, 1)
            bands.append(jnp.concatenate([wide[i, side, q] for q in range(q_count)], axis=1))
        matrix = jnp.concatenate([blocks[q, p] for q in range(q_count)], axis=1)
        image = dot_nt(jnp.concatenate(bands, axis=0), matrix).astype(BF16)
        for a in range(6):
            i, dp = around(p, a)
            inside = (2 * p - 2 + a == i) & (dp >= 0) & (dp <= 1)
            term = dot_nn(image[a * vecs:(a + 1) * vecs], left_ref[i, jnp.clip(dp, 0, 1)])
            partial[i] += term * jnp.where(inside, 1.0, 0.0)

    relay = pltpu.make_async_remote_copy(
        src_ref=blocks.at[:, 0], dst_ref=blocks.at[:, p_count - 1],
        send_sem=relay_send, recv_sem=relay_recv,
        device_id=(row_peer(n_rows - 1), col_id), device_id_type=MESH,
    )

    def near_copy(place):
        return pltpu.make_async_remote_copy(
            src_ref=blocks.at[0, place], dst_ref=blocks.at[coarse_cols, place],
            send_sem=near_send.at[place], recv_sem=rim_recv.at[place],
            device_id=(row_id, sibling), device_id_type=MESH,
        )

    def wait_rim(place):
        pltpu.make_async_remote_copy(
            src_ref=blocks.at[coarse_cols, place], dst_ref=blocks.at[coarse_cols, place],
            send_sem=rim_send.at[0], recv_sem=rim_recv.at[place],
            device_id=(row_id, sibling), device_id_type=MESH,
        ).wait_recv()

    def use(place):
        @pl.when(place == 0)
        def _():
            relay.start()

        contract(place)

    def take(row, offset):
        source = lax.rem(col_id // 2 + offset // 2, n_cols // 2) * 2 + lax.rem(core + offset, 2)
        place = source * held + row
        pltpu.make_async_remote_copy(
            src_ref=blocks.at[pl.ds(0, coarse_cols), place], dst_ref=blocks.at[pl.ds(0, coarse_cols), place],
            send_sem=main_send.at[0], recv_sem=main_recv.at[place],
            device_id=(row_id, source), device_id_type=MESH,
        ).wait_recv()

        @pl.when((core == 1) & (offset != 1))
        def _():
            near_copy(place).start()

        wait_rim(place)
        use(place)

    for copy in own:
        copy.wait()
    @pl.when(core == 1)
    def _():
        for row in range(held):
            near_copy(col_id * held + row).start()

    for row in range(held):
        use(col_id * held + row)

    def take_step(step, carry):
        take(step // (n_cols - 1), step % (n_cols - 1) + 1)
        return carry

    lax.fori_loop(0, held * (n_cols - 1), take_step, 0)
    relay.wait_recv()
    contract(p_count - 1)

    def part_copy(step):
        peer = column_peer(step)
        return pltpu.make_async_remote_copy(
            src_ref=part_out.at[peer], dst_ref=part_in.at[col_id],
            send_sem=part_send.at[step], recv_sem=part_recv.at[col_id],
            device_id=(row_id, peer), device_id_type=MESH,
        )

    def fill_part(target):
        for k in range(chunk):
            part_out[target, :, pl.ds(k * nb, nb)] = partial[target * chunk + k].astype(BF16)

    backwards = list(range(n_cols - 2, -1, -1))
    for step in backwards:
        fill_part(column_peer(step))
        part_copy(step).start()
    fill_part(col_id)

    total = part_out[col_id].astype(F32)
    for offset in range(1, n_cols):
        source = flip(col_id, offset)
        pltpu.make_async_remote_copy(
            src_ref=part_in.at[source], dst_ref=part_in.at[source],
            send_sem=part_send.at[0], recv_sem=part_recv.at[source],
            device_id=(row_id, source), device_id_type=MESH,
        ).wait_recv()
        total = total + part_in[source].astype(F32)
    image = total.astype(BF16)
    gathered[col_id] = image

    def row_copy(step):
        return pltpu.make_async_remote_copy(
            src_ref=gathered.at[col_id], dst_ref=gathered.at[col_id],
            send_sem=row_send.at[step], recv_sem=row_recv.at[col_id],
            device_id=(row_id, column_peer(step)), device_id_type=MESH,
        )

    for step in backwards:
        row_copy(step).start()
    forward_ref[...] = image

    def lift(source):
        for k in range(0, chunk, 2):
            bands = []
            for i in (source * chunk + k, source * chunk + k + 1):
                piece = gathered[source, :, pl.ds((k + len(bands)) * nb, nb)]
                bands.append(dot_nt(piece, left_ref[i].reshape(2 * nb, nb)).astype(BF16))
            for member in range(2):
                lifted[source * chunk + k + member, 0] = bands[member][:, :nb]
                lifted[source * chunk + k + member, 1] = bands[member][:, nb:]
            point = source * chunk + k
            above = point // 2
            for slot in range(3):
                p = above - 1 + slot
                picked = [
                    lifted[point + member, jnp.clip(p - row_base(point + member), 0, 1)] for member in range(2)
                ]
                place = jnp.maximum(p, 0)
                matrix = jnp.concatenate([blocks[q, place] for q in range(q_count)], axis=1)
                image = dot_nn(jnp.concatenate(picked, axis=0), matrix).astype(BF16)
                at = p * 6 + 6 + (2 - slot) * 2
                for member in range(2):
                    for q in range(q_count):
                        slots[at + member, q] = image[member * vecs:(member + 1) * vecs, q * nb:(q + 1) * nb]

    lift(col_id)

    def lift_next(step, carry):
        offset = step + 1
        source = lax.rem(col_id // 2 + offset // 2, n_cols // 2) * 2 + lax.rem(core + offset, 2)
        pltpu.make_async_remote_copy(
            src_ref=gathered.at[source], dst_ref=gathered.at[source],
            send_sem=row_send.at[0], recv_sem=row_recv.at[source],
            device_id=(row_id, source), device_id_type=MESH,
        ).wait_recv()
        lift(source)
        return carry

    lax.fori_loop(0, n_cols - 1, lift_next, 0)

    def back_copy(piece, offset):
        peer = row_peer(offset)
        return pltpu.make_async_remote_copy(
            src_ref=back_out.at[piece, peer], dst_ref=back_in.at[piece, row_id],
            send_sem=back_send.at[piece, offset], recv_sem=back_recv.at[piece, row_id],
            device_id=(peer, col_id), device_id_type=MESH,
        )

    pieces = back_out.shape[0]
    span = fine_cols // pieces
    group = 8
    for piece in range(pieces):
        def finish(step, carry):
            j = piece * span + step
            q = col_base(j)
            slot = 1 + q - j // 2

            def add(block, totals):
                first, second = totals
                for k in range(group):
                    i = block * group + k
                    at = spot[i]
                    for dp in range(2):
                        row = (j + 2) * 8 + slot + dp * 3
                        first = first + mix[row, i] * slots[at + 4 * dp, q].astype(F32)
                        second = second + mix[row + 1, i] * slots[at + 4 * dp, q + 1].astype(F32)
                return first, second

            zero = jnp.zeros((vecs, nb), F32)
            first, second = lax.fori_loop(0, fine_rows // group, add, (zero, zero))
            both = jnp.concatenate([first.astype(BF16), second.astype(BF16)], axis=1)
            image = dot_nn(both, right_ref[j].reshape(2 * nb, nb))
            for target in range(n_rows):
                back_out[piece, target, :, pl.ds(pl.multiple_of(step * nb, nb), nb)] = (
                    image[target * share:(target + 1) * share].astype(BF16)
                )
            return carry

        lax.fori_loop(0, span, finish, 0)
        for offset in range(1, n_rows):
            back_copy(piece, offset).start()

    for piece in range(pieces):
        total = back_out[piece, row_id].astype(F32)
        for offset in range(1, n_rows):
            source = row_peer(offset)
            pltpu.make_async_remote_copy(
                src_ref=back_in.at[piece, source], dst_ref=back_in.at[piece, source],
                send_sem=back_send.at[piece, 0], recv_sem=back_recv.at[piece, source],
                device_id=(source, col_id), device_id_type=MESH,
            ).wait_recv()
            total = total + back_in[piece, source].astype(F32)
        adjoint_ref[:, pl.ds(piece * span * nb, span * nb)] = total.astype(BF16)

    for copy in sends:
        copy.wait_send()
    for used, copy in rims:
        pl.when(used)(copy.wait_send)

    @pl.when(core == 1)
    def _():
        def settle(step, carry):
            row, offset = step // (n_cols - 1), step % (n_cols - 1)
            offset = offset + jnp.minimum(offset, 1)
            source = lax.rem(col_id // 2 + offset // 2, n_cols // 2) * 2 + lax.rem(core + offset, 2)
            near_copy(source * held + row).wait_send()
            return carry

        lax.fori_loop(0, held * (n_cols - 1), settle, 0)

    relay.wait_send()
    for step in range(n_cols - 1):
        part_copy(step).wait_send()
        row_copy(step).wait_send()
    for piece in range(pieces):
        for offset in range(1, n_rows):
            back_copy(piece, offset).wait_send()


def body(
    coarse_kernel,
    left_rotation,
    right_rotation,
    fine_map,
    coefficient_index,
    coefficient_table,
    trial_vectors,
):
    n_rows = lax.axis_size("rowk")
    n_cols = lax.axis_size("colk")
    held, coarse_total = coarse_kernel.shape[:2]
    fine_rows = left_rotation.shape[0]
    fine_cols = right_rotation.shape[0]
    nb = left_rotation.shape[2]
    vecs = trial_vectors.shape[0]
    p_count = coarse_total // n_rows + 1
    q_count = coarse_total // n_cols + 1
    chunk = fine_rows // n_cols
    share = vecs // n_rows
    pieces = 2

    sizes = (n_rows, n_cols, held, p_count, q_count, fine_rows, fine_cols, nb, vecs)
    anywhere = pl.BlockSpec(memory_space=pltpu.HBM)
    vmem = pl.BlockSpec(memory_space=pltpu.VMEM)
    smem = pl.BlockSpec(memory_space=pltpu.SMEM)
    dma = pltpu.SemaphoreType.DMA
    return pl.pallas_call(
        functools.partial(operator_kernel, sizes),
        out_shape=(
            jax.ShapeDtypeStruct((vecs, chunk * nb), BF16),
            jax.ShapeDtypeStruct((share, fine_cols * nb), BF16),
        ),
        in_specs=[anywhere, anywhere, anywhere, smem, vmem, smem, anywhere],
        out_specs=(vmem, vmem),
        scratch_shapes=[
            pltpu.VMEM((q_count, p_count, nb, nb), BF16),
            pltpu.VMEM((fine_cols + 6, 3, vecs, nb), F32),
            pltpu.VMEM((fine_rows, 2, q_count, vecs, nb), BF16),
            pltpu.VMEM((fine_rows, vecs, nb), F32),
            pltpu.VMEM((n_cols, vecs, chunk * nb), BF16),
            pltpu.VMEM((n_cols, vecs, chunk * nb), BF16),
            pltpu.VMEM((n_cols, vecs, chunk * nb), BF16),
            pltpu.VMEM((fine_rows, 2, vecs, nb), BF16),
            pltpu.VMEM((p_count * 6 + 6, q_count, vecs, nb), BF16),
            pltpu.VMEM((pieces, n_rows, share, fine_cols * nb // pieces), BF16),
            pltpu.VMEM((pieces, n_rows, share, fine_cols * nb // pieces), BF16),
            pltpu.VMEM(left_rotation.shape, BF16),
            pltpu.VMEM(right_rotation.shape, BF16),
            pltpu.VMEM(trial_vectors.shape, BF16),
            pltpu.VMEM(((fine_cols + 6) * 8, 128), F32),
            pltpu.SMEM(((fine_cols + 6) * 8, 128), F32),
            pltpu.SMEM((fine_rows,), jnp.int32),
            dma((held, 2)),
            dma((3,)),
            dma(()),
            dma((held * n_cols,)),
            dma((p_count,)),
            dma((held * n_cols,)),
            dma((p_count,)),
            dma((p_count,)),
            dma(()),
            dma(()),
            dma((n_cols,)),
            dma((n_cols,)),
            dma((n_cols,)),
            dma((n_cols,)),
            dma((pieces, n_rows)),
            dma((pieces, n_rows)),
        ],
        compiler_params=pltpu.CompilerParams(
            collective_id=0, has_side_effects=True, vmem_limit_bytes=52 * 1024 * 1024
        ),
        name="operator_images",
    )(
        coarse_kernel, left_rotation, right_rotation, fine_map, coefficient_index.transpose(1, 2, 0),
        coefficient_table, trial_vectors
    )


def solution(mesh):
    return jax.shard_map(
        body,
        mesh=mesh,
        in_specs=(
            P(("rowk", "colk"), None, None, None),
            P("rowk", None, None, None),
            P("colk", None, None, None),
            P(),
            P("rowk", "colk", None),
            P(),
            P(None, "colk"),
        ),
        out_specs=(P(None, ("rowk", "colk")), P("rowk", "colk")),
        check_vma=False,
    )
```

```python
import functools

import jax
import jax.numpy as jnp
from jax import lax
from jax.experimental import pallas as pl
from jax.experimental.pallas import tpu as pltpu
from jax.sharding import PartitionSpec as P

MESH = pl.DeviceIdType.MESH
F32 = jnp.float32
BF16 = jnp.bfloat16


def dot_nt(left, right):
    return lax.dot_general(left, right, (((1,), (1,)), ((), ())), preferred_element_type=F32)


def dot_nn(left, right):
    return lax.dot_general(left, right, (((1,), (0,)), ((), ())), preferred_element_type=F32)


def flip(index, bits):
    out, place = index, 1
    while place <= bits:
        if bits & place:
            out = out + place * (1 - 2 * (index // place % 2))
        place *= 2
    return out


def operator_kernel(
    sizes,
    kernel_ref, left_far, right_far, map_ref, index_ref, table_ref, vec_far,
    forward_ref, adjoint_ref,
    blocks, turned, wide, partial, part_out, part_in, gathered, lifted, slots,
    back_out, back_in, left_ref, right_ref, vec_ref, mix_rows, mix, spot,
    own_sem, load_sem, mix_sem, main_send, main_recv, rim_send, rim_recv, near_send, relay_send, relay_recv,
    part_send, part_recv, row_send, row_recv, back_send, back_recv,
):
    n_rows, n_cols, held, p_count, q_count, fine_rows, fine_cols, nb, vecs = sizes
    row_id, col_id = lax.axis_index("rowk"), lax.axis_index("colk")
    coarse_cols = q_count - 1
    chunk = fine_rows // n_cols
    share = vecs // n_rows
    j_pad = fine_cols + 6
    core = col_id % 2
    sibling = flip(col_id, 1)

    far = list(range(2, n_cols))
    orders = ([1] + far, [1] + far[2:4] + far[:2] + far[4:])

    def column_peer(step):
        first, second = orders[0][step], orders[1][step]
        return (1 - core) * flip(col_id, first) + core * flip(col_id, second)

    def row_peer(offset):
        return lax.rem(row_id + offset, n_rows)

    barrier = pltpu.get_barrier_semaphore()
    for offset in range(1, n_cols):
        pl.semaphore_signal(barrier, inc=1, device_id=(row_id, flip(col_id, offset)), device_id_type=MESH)
    for offset in range(1, n_rows):
        pl.semaphore_signal(barrier, inc=1, device_id=(row_peer(offset), col_id), device_id_type=MESH)
    pl.semaphore_wait(barrier, n_cols - 1 + n_rows - 1)

    far_count = n_cols - 2
    window = 4
    copies = held * far_count

    def far_peer(at, turn_of):
        step = at % far_count
        chip, other = step // 2, step % 2
        first = jnp.where(chip < 2, 1 - chip, chip) * turn_of + chip * (1 - turn_of) + 1
        mine, found, place = col_id // 2, 0, 1
        while place < n_cols // 2:
            left, right = first // place % 2, mine // place % 2
            found = found + place * (left + right - 2 * left * right)
            place *= 2
        return found * 2 + core + other * (1 - 2 * core)

    def coarse_copy(row, peer, at):
        return pltpu.make_async_remote_copy(
            src_ref=kernel_ref.at[row, pl.ds(peer * coarse_cols, coarse_cols)],
            dst_ref=blocks.at[pl.ds(0, coarse_cols), col_id * held + row],
            send_sem=main_send.at[at], recv_sem=main_recv.at[col_id * held + row],
            device_id=(row_id, peer), device_id_type=MESH,
        )

    def edge_copy(row, peer, at):
        rim = lax.rem(peer + 1, n_cols) * coarse_cols
        return pltpu.make_async_remote_copy(
            src_ref=kernel_ref.at[row, rim], dst_ref=blocks.at[coarse_cols, col_id * held + row],
            send_sem=rim_send.at[at], recv_sem=rim_recv.at[col_id * held + row],
            device_id=(row_id, peer), device_id_type=MESH,
        )

    def start_far(at):
        peer = far_peer(at, core)
        row = at // far_count
        coarse_copy(row, peer, at).start()

        @pl.when(peer % 2 == 1)
        def _():
            edge_copy(row, peer, at).start()

    def wait_far(at):
        peer = far_peer(at, core)
        row = at // far_count
        coarse_copy(row, peer, at).wait_send()

        @pl.when(peer % 2 == 1)
        def _():
            edge_copy(row, peer, at).wait_send()

    def advance(at):
        wait_far(at)
        start_far(at + window)

    for at in range(window):
        start_far(at)
    for row in range(held):
        coarse_copy(row, sibling, copies + row).start()

    @pl.when(core == 0)
    def _():
        for row in range(held):
            edge_copy(row, sibling, copies + row).start()

    own = []
    for row in range(held):
        place = col_id * held + row
        rim = lax.rem(col_id + 1, n_cols) * coarse_cols
        own.append(pltpu.make_async_copy(
            kernel_ref.at[row, pl.ds(col_id * coarse_cols, coarse_cols)],
            blocks.at[pl.ds(0, coarse_cols), place], own_sem.at[row, 0],
        ))
        own.append(pltpu.make_async_copy(
            kernel_ref.at[row, rim], blocks.at[coarse_cols, place], own_sem.at[row, 1],
        ))
    for copy in own:
        copy.start()
    loads = [
        pltpu.make_async_copy(far_ref, near_ref, load_sem.at[at])
        for at, (far_ref, near_ref) in enumerate(((vec_far, vec_ref), (right_far, right_ref), (left_far, left_ref)))
    ]
    for copy in loads:
        copy.start()

    def row_base(i):
        base = map_ref[row_id * fine_rows + i] - row_id * (p_count - 1)
        return jnp.clip(base, jnp.maximum(i // 2 - 1, 0), i // 2)

    def col_base(j):
        base = map_ref[col_id * fine_cols + j] - col_id * coarse_cols
        return jnp.clip(base, jnp.maximum(j // 2 - 1, 0), j // 2)

    mix_rows[...] = jnp.zeros_like(mix_rows)

    def weigh(j, carry):
        entry = index_ref[j]
        weight = jnp.zeros(entry.shape, F32)
        for k in range(1, table_ref.shape[0]):
            weight = jnp.where(entry == k, table_ref[k], weight)
        lower = jnp.where(col_base(j) < j // 2, 1.0, 0.0)
        for dp in range(2):
            near, next_one = weight[2 * dp:2 * dp + 1], weight[2 * dp + 1:2 * dp + 2]
            values = (lower * near, lower * next_one + (1.0 - lower) * near, (1.0 - lower) * next_one)
            for slot in range(3):
                mix_rows[pl.ds((j + 2) * 8 + dp * 3 + slot, 1), pl.ds(0, fine_rows)] = values[slot]
        return carry

    lax.fori_loop(0, fine_cols, weigh, 0)
    mix_copy = pltpu.make_async_copy(mix_rows, mix, mix_sem)
    mix_copy.start()

    def locate(i, carry):
        spot[i] = 4 * row_base(i) + i + 8
        return carry

    lax.fori_loop(0, fine_rows, locate, 0)

    turned[...] = jnp.zeros_like(turned)
    partial[...] = jnp.zeros_like(partial)

    def turn(j, carry):
        vec = vec_ref[:, pl.ds(pl.multiple_of(j * nb, nb), nb)]
        for slot in range(3):
            side = jnp.clip(j // 2 - 1 + slot - col_base(j), 0, 1)
            turned[j + 2, slot] = dot_nt(vec, right_ref[j, side])
        return carry

    for copy in loads:
        copy.wait()
    lax.fori_loop(0, fine_cols, turn, 0)
    mix_copy.wait()

    half = vecs // 2

    def widen(q, pair, count):
        for part in range(2):
            rows = pl.ds(part * half, half)
            tiles = [turned[2 * q + b, 2 - b // 2, rows] for b in range(count)]
            for k in range(2):
                for dp in range(2):
                    i = 2 * pair + k
                    total = mix[2 * q * 8 + dp * 3 + 2, i] * tiles[0]
                    for b in range(1, count):
                        total += mix[(2 * q + b) * 8 + dp * 3 + 2 - b // 2, i] * tiles[b]
                    wide[i, dp, q, rows] = total.astype(BF16)

    pairs = fine_rows // 2

    def widen_step(step, carry):
        widen(step // pairs, step % pairs, 6)
        return carry

    def widen_last(pair, carry):
        widen(coarse_cols, pair, 2)
        return carry

    early = 3
    bounds = [0] + [(coarse_cols - early + k + 1) * pairs for k in range(early)]
    for k in range(early):
        lax.fori_loop(bounds[k], bounds[k + 1], widen_step, 0)
        advance(k)
    lax.fori_loop(0, pairs, widen_last, 0)

    def around(p, a):
        i = jnp.clip(2 * p - 2 + a, 0, fine_rows - 1)
        return i, p - row_base(i)

    def contract(p):
        bands = []
        for a in range(6):
            i, dp = around(p, a)
            side = jnp.clip(dp, 0, 1)
            bands.append(jnp.concatenate([wide[i, side, q] for q in range(q_count)], axis=1))
        matrix = jnp.concatenate([blocks[q, p] for q in range(q_count)], axis=1)
        image = dot_nt(jnp.concatenate(bands, axis=0), matrix).astype(BF16)
        for a in range(6):
            i, dp = around(p, a)
            inside = (2 * p - 2 + a == i) & (dp >= 0) & (dp <= 1)
            term = dot_nn(image[a * vecs:(a + 1) * vecs], left_ref[i, jnp.clip(dp, 0, 1)])
            partial[i] += term * jnp.where(inside, 1.0, 0.0)

    relay = pltpu.make_async_remote_copy(
        src_ref=blocks.at[:, 0], dst_ref=blocks.at[:, p_count - 1],
        send_sem=relay_send, recv_sem=relay_recv,
        device_id=(row_peer(n_rows - 1), col_id), device_id_type=MESH,
    )

    def near_copy(place):
        return pltpu.make_async_remote_copy(
            src_ref=blocks.at[0, place], dst_ref=blocks.at[coarse_cols, place],
            send_sem=near_send.at[place], recv_sem=rim_recv.at[place],
            device_id=(row_id, sibling), device_id_type=MESH,
        )

    def wait_rim(place):
        pltpu.make_async_remote_copy(
            src_ref=blocks.at[coarse_cols, place], dst_ref=blocks.at[coarse_cols, place],
            send_sem=rim_send.at[0], recv_sem=rim_recv.at[place],
            device_id=(row_id, sibling), device_id_type=MESH,
        ).wait_recv()

    def use(place):
        @pl.when(place == 0)
        def _():
            relay.start()

        contract(place)

    def take(row, source):
        place = source * held + row
        pltpu.make_async_remote_copy(
            src_ref=blocks.at[pl.ds(0, coarse_cols), place], dst_ref=blocks.at[pl.ds(0, coarse_cols), place],
            send_sem=main_send.at[0], recv_sem=main_recv.at[place],
            device_id=(row_id, source), device_id_type=MESH,
        ).wait_recv()

        @pl.when((core == 1) & (source != sibling))
        def _():
            near_copy(place).start()

        wait_rim(place)
        use(place)

    for copy in own:
        copy.wait()
    @pl.when(core == 1)
    def _():
        for row in range(held):
            near_copy(col_id * held + row).start()

    for row in range(held):
        use(col_id * held + row)

    for row in range(held):
        take(row, sibling)

    def take_step(at, carry):
        @pl.when(at + early < copies - window)
        def _():
            advance(at + early)

        take(at // far_count, far_peer(at, core))
        return carry

    lax.fori_loop(0, copies, take_step, 0)
    relay.wait_recv()
    contract(p_count - 1)

    def part_copy(step):
        peer = column_peer(step)
        return pltpu.make_async_remote_copy(
            src_ref=part_out.at[peer], dst_ref=part_in.at[col_id],
            send_sem=part_send.at[step], recv_sem=part_recv.at[col_id],
            device_id=(row_id, peer), device_id_type=MESH,
        )

    def fill_part(target):
        for k in range(chunk):
            part_out[target, :, pl.ds(k * nb, nb)] = partial[target * chunk + k].astype(BF16)

    backwards = list(range(n_cols - 2, -1, -1))
    for step in backwards:
        fill_part(column_peer(step))
        part_copy(step).start()
    fill_part(col_id)

    total = part_out[col_id].astype(F32)
    for offset in range(1, n_cols):
        source = flip(col_id, offset)
        pltpu.make_async_remote_copy(
            src_ref=part_in.at[source], dst_ref=part_in.at[source],
            send_sem=part_send.at[0], recv_sem=part_recv.at[source],
            device_id=(row_id, source), device_id_type=MESH,
        ).wait_recv()
        total = total + part_in[source].astype(F32)
    image = total.astype(BF16)
    gathered[col_id] = image

    def row_copy(step):
        return pltpu.make_async_remote_copy(
            src_ref=gathered.at[col_id], dst_ref=gathered.at[col_id],
            send_sem=row_send.at[step], recv_sem=row_recv.at[col_id],
            device_id=(row_id, column_peer(step)), device_id_type=MESH,
        )

    for step in backwards:
        row_copy(step).start()
    forward_ref[...] = image

    def lift(source):
        for k in range(0, chunk, 2):
            bands = []
            for i in (source * chunk + k, source * chunk + k + 1):
                piece = gathered[source, :, pl.ds((k + len(bands)) * nb, nb)]
                bands.append(dot_nt(piece, left_ref[i].reshape(2 * nb, nb)).astype(BF16))
            for member in range(2):
                lifted[source * chunk + k + member, 0] = bands[member][:, :nb]
                lifted[source * chunk + k + member, 1] = bands[member][:, nb:]
            point = source * chunk + k
            above = point // 2
            for slot in range(3):
                p = above - 1 + slot
                picked = [
                    lifted[point + member, jnp.clip(p - row_base(point + member), 0, 1)] for member in range(2)
                ]
                place = jnp.maximum(p, 0)
                matrix = jnp.concatenate([blocks[q, place] for q in range(q_count)], axis=1)
                image = dot_nn(jnp.concatenate(picked, axis=0), matrix).astype(BF16)
                at = p * 6 + 6 + (2 - slot) * 2
                for member in range(2):
                    for q in range(q_count):
                        slots[at + member, q] = image[member * vecs:(member + 1) * vecs, q * nb:(q + 1) * nb]

    lift(col_id)

    def lift_next(step, carry):
        offset = step + 1
        source = lax.rem(col_id // 2 + offset // 2, n_cols // 2) * 2 + lax.rem(core + offset, 2)
        pltpu.make_async_remote_copy(
            src_ref=gathered.at[source], dst_ref=gathered.at[source],
            send_sem=row_send.at[0], recv_sem=row_recv.at[source],
            device_id=(row_id, source), device_id_type=MESH,
        ).wait_recv()
        lift(source)
        return carry

    lax.fori_loop(0, n_cols - 1, lift_next, 0)

    def back_copy(piece, offset):
        peer = row_peer(offset)
        return pltpu.make_async_remote_copy(
            src_ref=back_out.at[piece, peer], dst_ref=back_in.at[piece, row_id],
            send_sem=back_send.at[piece, offset], recv_sem=back_recv.at[piece, row_id],
            device_id=(peer, col_id), device_id_type=MESH,
        )

    pieces = back_out.shape[0]
    span = fine_cols // pieces
    group = 8
    for piece in range(pieces):
        def finish(step, carry):
            j = piece * span + step
            q = col_base(j)
            slot = 1 + q - j // 2

            def add(block, totals):
                first, second = totals
                for k in range(group):
                    i = block * group + k
                    at = spot[i]
                    for dp in range(2):
                        row = (j + 2) * 8 + slot + dp * 3
                        first = first + mix[row, i] * slots[at + 4 * dp, q].astype(F32)
                        second = second + mix[row + 1, i] * slots[at + 4 * dp, q + 1].astype(F32)
                return first, second

            zero = jnp.zeros((vecs, nb), F32)
            first, second = lax.fori_loop(0, fine_rows // group, add, (zero, zero))
            both = jnp.concatenate([first.astype(BF16), second.astype(BF16)], axis=1)
            image = dot_nn(both, right_ref[j].reshape(2 * nb, nb))
            for target in range(n_rows):
                back_out[piece, target, :, pl.ds(pl.multiple_of(step * nb, nb), nb)] = (
                    image[target * share:(target + 1) * share].astype(BF16)
                )
            return carry

        lax.fori_loop(0, span, finish, 0)
        for offset in range(1, n_rows):
            back_copy(piece, offset).start()

    for piece in range(pieces):
        total = back_out[piece, row_id].astype(F32)
        for offset in range(1, n_rows):
            source = row_peer(offset)
            pltpu.make_async_remote_copy(
                src_ref=back_in.at[piece, source], dst_ref=back_in.at[piece, source],
                send_sem=back_send.at[piece, 0], recv_sem=back_recv.at[piece, source],
                device_id=(source, col_id), device_id_type=MESH,
            ).wait_recv()
            total = total + back_in[piece, source].astype(F32)
        adjoint_ref[:, pl.ds(piece * span * nb, span * nb)] = total.astype(BF16)

    for row in range(held):
        coarse_copy(row, sibling, copies + row).wait_send()

    @pl.when(core == 0)
    def _():
        for row in range(held):
            edge_copy(row, sibling, copies + row).wait_send()

    def settle(at, carry):
        wait_far(at)
        return carry

    lax.fori_loop(copies - window, copies, settle, 0)

    @pl.when(core == 1)
    def _():
        for row in range(held):
            near_copy(col_id * held + row).wait_send()

        def settle_near(at, carry):
            near_copy(far_peer(at, core) * held + at // far_count).wait_send()
            return carry

        lax.fori_loop(0, copies, settle_near, 0)

    relay.wait_send()
    for step in range(n_cols - 1):
        part_copy(step).wait_send()
        row_copy(step).wait_send()
    for piece in range(pieces):
        for offset in range(1, n_rows):
            back_copy(piece, offset).wait_send()


def body(
    coarse_kernel,
    left_rotation,
    right_rotation,
    fine_map,
    coefficient_index,
    coefficient_table,
    trial_vectors,
):
    n_rows = lax.axis_size("rowk")
    n_cols = lax.axis_size("colk")
    held, coarse_total = coarse_kernel.shape[:2]
    fine_rows = left_rotation.shape[0]
    fine_cols = right_rotation.shape[0]
    nb = left_rotation.shape[2]
    vecs = trial_vectors.shape[0]
    p_count = coarse_total // n_rows + 1
    q_count = coarse_total // n_cols + 1
    chunk = fine_rows // n_cols
    share = vecs // n_rows
    pieces = 4

    sizes = (n_rows, n_cols, held, p_count, q_count, fine_rows, fine_cols, nb, vecs)
    anywhere = pl.BlockSpec(memory_space=pltpu.HBM)
    vmem = pl.BlockSpec(memory_space=pltpu.VMEM)
    smem = pl.BlockSpec(memory_space=pltpu.SMEM)
    dma = pltpu.SemaphoreType.DMA
    return pl.pallas_call(
        functools.partial(operator_kernel, sizes),
        out_shape=(
            jax.ShapeDtypeStruct((vecs, chunk * nb), BF16),
            jax.ShapeDtypeStruct((share, fine_cols * nb), BF16),
        ),
        in_specs=[anywhere, anywhere, anywhere, smem, vmem, smem, anywhere],
        out_specs=(vmem, vmem),
        scratch_shapes=[
            pltpu.VMEM((q_count, p_count, nb, nb), BF16),
            pltpu.VMEM((fine_cols + 6, 3, vecs, nb), F32),
            pltpu.VMEM((fine_rows, 2, q_count, vecs, nb), BF16),
            pltpu.VMEM((fine_rows, vecs, nb), F32),
            pltpu.VMEM((n_cols, vecs, chunk * nb), BF16),
            pltpu.VMEM((n_cols, vecs, chunk * nb), BF16),
            pltpu.VMEM((n_cols, vecs, chunk * nb), BF16),
            pltpu.VMEM((fine_rows, 2, vecs, nb), BF16),
            pltpu.VMEM((p_count * 6 + 6, q_count, vecs, nb), BF16),
            pltpu.VMEM((pieces, n_rows, share, fine_cols * nb // pieces), BF16),
            pltpu.VMEM((pieces, n_rows, share, fine_cols * nb // pieces), BF16),
            pltpu.VMEM(left_rotation.shape, BF16),
            pltpu.VMEM(right_rotation.shape, BF16),
            pltpu.VMEM(trial_vectors.shape, BF16),
            pltpu.VMEM(((fine_cols + 6) * 8, 128), F32),
            pltpu.SMEM(((fine_cols + 6) * 8, 128), F32),
            pltpu.SMEM((fine_rows,), jnp.int32),
            dma((held, 2)),
            dma((3,)),
            dma(()),
            dma((held * n_cols,)),
            dma((p_count,)),
            dma((held * n_cols,)),
            dma((p_count,)),
            dma((p_count,)),
            dma(()),
            dma(()),
            dma((n_cols,)),
            dma((n_cols,)),
            dma((n_cols,)),
            dma((n_cols,)),
            dma((pieces, n_rows)),
            dma((pieces, n_rows)),
        ],
        compiler_params=pltpu.CompilerParams(
            collective_id=0, has_side_effects=True, vmem_limit_bytes=52 * 1024 * 1024
        ),
        name="operator_images",
    )(
        coarse_kernel, left_rotation, right_rotation, fine_map, coefficient_index.transpose(1, 2, 0),
        coefficient_table, trial_vectors
    )


def solution(mesh):
    return jax.shard_map(
        body,
        mesh=mesh,
        in_specs=(
            P(("rowk", "colk"), None, None, None),
            P("rowk", None, None, None),
            P("colk", None, None, None),
            P(),
            P("rowk", "colk", None),
            P(),
            P(None, "colk"),
        ),
        out_specs=(P(None, ("rowk", "colk")), P("rowk", "colk")),
        check_vma=False,
    )
```

```python
import functools

import jax
import jax.numpy as jnp
from jax import lax
from jax.experimental import pallas as pl
from jax.experimental.pallas import tpu as pltpu
from jax.sharding import PartitionSpec as P

MESH = pl.DeviceIdType.MESH
F32 = jnp.float32
BF16 = jnp.bfloat16


def dot_nt(left, right):
    return lax.dot_general(left, right, (((1,), (1,)), ((), ())), preferred_element_type=F32)


def dot_nn(left, right):
    return lax.dot_general(left, right, (((1,), (0,)), ((), ())), preferred_element_type=F32)


def flip(index, bits):
    out, place = index, 1
    while place <= bits:
        if bits & place:
            out = out + place * (1 - 2 * (index // place % 2))
        place *= 2
    return out


def operator_kernel(
    sizes,
    kernel_ref, left_far, right_far, map_ref, index_ref, table_ref, vec_far,
    forward_ref, adjoint_ref,
    blocks, turned, wide, partial, part_out, part_in, gathered, lifted, slots,
    back_out, back_in, left_ref, right_ref, vec_ref, mix_rows, mix, spot,
    own_sem, load_sem, mix_sem, main_send, main_recv, rim_send, rim_recv, near_send, relay_send, relay_recv,
    part_send, part_recv, row_send, row_recv, back_send, back_recv,
):
    n_rows, n_cols, held, p_count, q_count, fine_rows, fine_cols, nb, vecs = sizes
    row_id, col_id = lax.axis_index("rowk"), lax.axis_index("colk")
    coarse_cols = q_count - 1
    chunk = fine_rows // n_cols
    share = vecs // n_rows
    j_pad = fine_cols + 6
    core = col_id % 2
    sibling = flip(col_id, 1)

    far = list(range(2, n_cols))
    orders = ([1] + far, [1] + far[2:4] + far[:2] + far[4:])

    def column_peer(step):
        first, second = orders[0][step], orders[1][step]
        return (1 - core) * flip(col_id, first) + core * flip(col_id, second)

    def row_peer(offset):
        return lax.rem(row_id + offset, n_rows)

    barrier = pltpu.get_barrier_semaphore()
    for offset in range(1, n_cols):
        pl.semaphore_signal(barrier, inc=1, device_id=(row_id, flip(col_id, offset)), device_id_type=MESH)
    for offset in range(1, n_rows):
        pl.semaphore_signal(barrier, inc=1, device_id=(row_peer(offset), col_id), device_id_type=MESH)
    pl.semaphore_wait(barrier, n_cols - 1 + n_rows - 1)

    sends = []
    rims = []
    for row in range(held):
        place = col_id * held + row
        for step in range(n_cols - 1):
            peer = column_peer(step)
            rim = lax.rem(peer + 1, n_cols) * coarse_cols
            at = row * n_cols + step
            main = pltpu.make_async_remote_copy(
                src_ref=kernel_ref.at[row, pl.ds(peer * coarse_cols, coarse_cols)],
                dst_ref=blocks.at[pl.ds(0, coarse_cols), place],
                send_sem=main_send.at[at], recv_sem=main_recv.at[place],
                device_id=(row_id, peer), device_id_type=MESH,
            )
            edge = pltpu.make_async_remote_copy(
                src_ref=kernel_ref.at[row, rim], dst_ref=blocks.at[coarse_cols, place],
                send_sem=rim_send.at[at], recv_sem=rim_recv.at[place],
                device_id=(row_id, peer), device_id_type=MESH,
            )
            sends.append(main)
            main.start()
            rims.append((peer % 2 == 1, edge))
            pl.when(peer % 2 == 1)(edge.start)
    own = []
    for row in range(held):
        place = col_id * held + row
        rim = lax.rem(col_id + 1, n_cols) * coarse_cols
        own.append(pltpu.make_async_copy(
            kernel_ref.at[row, pl.ds(col_id * coarse_cols, coarse_cols)],
            blocks.at[pl.ds(0, coarse_cols), place], own_sem.at[row, 0],
        ))
        own.append(pltpu.make_async_copy(
            kernel_ref.at[row, rim], blocks.at[coarse_cols, place], own_sem.at[row, 1],
        ))
    for copy in own:
        copy.start()
    loads = [
        pltpu.make_async_copy(far_ref, near_ref, load_sem.at[at])
        for at, (far_ref, near_ref) in enumerate(((vec_far, vec_ref), (right_far, right_ref), (left_far, left_ref)))
    ]
    for copy in loads:
        copy.start()

    def row_base(i):
        base = map_ref[row_id * fine_rows + i] - row_id * (p_count - 1)
        return jnp.clip(base, jnp.maximum(i // 2 - 1, 0), i // 2)

    def col_base(j):
        base = map_ref[col_id * fine_cols + j] - col_id * coarse_cols
        return jnp.clip(base, jnp.maximum(j // 2 - 1, 0), j // 2)

    mix_rows[...] = jnp.zeros_like(mix_rows)

    def weigh(j, carry):
        entry = index_ref[j]
        weight = jnp.zeros(entry.shape, F32)
        for k in range(1, table_ref.shape[0]):
            weight = jnp.where(entry == k, table_ref[k], weight)
        lower = jnp.where(col_base(j) < j // 2, 1.0, 0.0)
        for dp in range(2):
            near, next_one = weight[2 * dp:2 * dp + 1], weight[2 * dp + 1:2 * dp + 2]
            values = (lower * near, lower * next_one + (1.0 - lower) * near, (1.0 - lower) * next_one)
            for slot in range(3):
                mix_rows[pl.ds((j + 2) * 8 + dp * 3 + slot, 1), pl.ds(0, fine_rows)] = values[slot]
        return carry

    lax.fori_loop(0, fine_cols, weigh, 0)
    mix_copy = pltpu.make_async_copy(mix_rows, mix, mix_sem)
    mix_copy.start()

    def locate(i, carry):
        spot[i] = 4 * row_base(i) + i + 8
        return carry

    lax.fori_loop(0, fine_rows, locate, 0)

    turned[...] = jnp.zeros_like(turned)

    def turn(j, carry):
        vec = vec_ref[:, pl.ds(pl.multiple_of(j * nb, nb), nb)]
        both = dot_nt(vec, right_ref[j].reshape(2 * nb, nb))
        turned[j + 2, 0] = both[:, :nb]
        turned[j + 2, 1] = jnp.where(col_base(j) < j // 2, both[:, nb:], both[:, :nb])
        turned[j + 2, 2] = both[:, nb:]
        return carry

    for copy in loads:
        copy.wait()
    lax.fori_loop(0, fine_cols, turn, 0)
    mix_copy.wait()

    half = vecs // 2

    def widen(q, pair, count):
        for part in range(2):
            rows = pl.ds(part * half, half)
            tiles = [turned[2 * q + b, 2 - b // 2, rows] for b in range(count)]
            for k in range(2):
                for dp in range(2):
                    i = 2 * pair + k
                    total = mix[2 * q * 8 + dp * 3 + 2, i] * tiles[0]
                    for b in range(1, count):
                        total += mix[(2 * q + b) * 8 + dp * 3 + 2 - b // 2, i] * tiles[b]
                    wide[i, dp, q, rows] = total.astype(BF16)

    pairs = fine_rows // 2

    def widen_step(step, carry):
        widen(step // pairs, step % pairs, 6)
        return carry

    def widen_last(pair, carry):
        widen(coarse_cols, pair, 2)
        return carry

    lax.fori_loop(0, coarse_cols * pairs, widen_step, 0)
    lax.fori_loop(0, pairs, widen_last, 0)

    def around(p, a):
        i = jnp.clip(2 * p - 2 + a, 0, fine_rows - 1)
        return i, p - row_base(i)

    def contract(p):
        bands = []
        for a in range(6):
            i, dp = around(p, a)
            side = jnp.clip(dp, 0, 1)
            bands.append(jnp.concatenate([wide[i, side, q] for q in range(q_count)], axis=1))
        matrix = jnp.concatenate([blocks[q, p] for q in range(q_count)], axis=1)
        image = dot_nt(jnp.concatenate(bands, axis=0), matrix).astype(BF16)
        for a in range(6):
            partial[p * 6 + a] = image[a * vecs:(a + 1) * vecs]

    relay = pltpu.make_async_remote_copy(
        src_ref=blocks.at[:, 0], dst_ref=blocks.at[:, p_count - 1],
        send_sem=relay_send, recv_sem=relay_recv,
        device_id=(row_peer(n_rows - 1), col_id), device_id_type=MESH,
    )

    def near_copy(place):
        return pltpu.make_async_remote_copy(
            src_ref=blocks.at[0, place], dst_ref=blocks.at[coarse_cols, place],
            send_sem=near_send.at[place], recv_sem=rim_recv.at[place],
            device_id=(row_id, sibling), device_id_type=MESH,
        )

    def wait_rim(place):
        pltpu.make_async_remote_copy(
            src_ref=blocks.at[coarse_cols, place], dst_ref=blocks.at[coarse_cols, place],
            send_sem=rim_send.at[0], recv_sem=rim_recv.at[place],
            device_id=(row_id, sibling), device_id_type=MESH,
        ).wait_recv()

    def use(place):
        @pl.when(place == 0)
        def _():
            relay.start()

        contract(place)

    def take(row, offset):
        source = lax.rem(col_id // 2 + offset // 2, n_cols // 2) * 2 + lax.rem(core + offset, 2)
        place = source * held + row
        pltpu.make_async_remote_copy(
            src_ref=blocks.at[pl.ds(0, coarse_cols), place], dst_ref=blocks.at[pl.ds(0, coarse_cols), place],
            send_sem=main_send.at[0], recv_sem=main_recv.at[place],
            device_id=(row_id, source), device_id_type=MESH,
        ).wait_recv()

        @pl.when((core == 1) & (offset != 1))
        def _():
            near_copy(place).start()

        wait_rim(place)
        use(place)

    for copy in own:
        copy.wait()
    @pl.when(core == 1)
    def _():
        for row in range(held):
            near_copy(col_id * held + row).start()

    for row in range(held):
        use(col_id * held + row)

    def take_step(step, carry):
        take(step // (n_cols - 1), step % (n_cols - 1) + 1)
        return carry

    lax.fori_loop(0, held * (n_cols - 1), take_step, 0)
    relay.wait_recv()
    contract(p_count - 1)

    def part_copy(step):
        peer = column_peer(step)
        return pltpu.make_async_remote_copy(
            src_ref=part_out.at[peer], dst_ref=part_in.at[col_id],
            send_sem=part_send.at[step], recv_sem=part_recv.at[col_id],
            device_id=(row_id, peer), device_id_type=MESH,
        )

    def fill_part(target):
        for k in range(chunk):
            i = target * chunk + k
            at = spot[i] - 6
            pair = jnp.concatenate([partial[at], partial[at + 4]], axis=1)
            part_out[target, :, pl.ds(k * nb, nb)] = dot_nn(pair, left_ref[i].reshape(2 * nb, nb)).astype(BF16)

    backwards = list(range(n_cols - 2, -1, -1))
    for step in backwards:
        fill_part(column_peer(step))
        part_copy(step).start()
    fill_part(col_id)

    total = part_out[col_id].astype(F32)
    for offset in range(1, n_cols):
        source = flip(col_id, offset)
        pltpu.make_async_remote_copy(
            src_ref=part_in.at[source], dst_ref=part_in.at[source],
            send_sem=part_send.at[0], recv_sem=part_recv.at[source],
            device_id=(row_id, source), device_id_type=MESH,
        ).wait_recv()
        total = total + part_in[source].astype(F32)
    image = total.astype(BF16)
    gathered[col_id] = image

    def row_copy(step):
        return pltpu.make_async_remote_copy(
            src_ref=gathered.at[col_id], dst_ref=gathered.at[col_id],
            send_sem=row_send.at[step], recv_sem=row_recv.at[col_id],
            device_id=(row_id, column_peer(step)), device_id_type=MESH,
        )

    for step in backwards:
        row_copy(step).start()
    forward_ref[...] = image

    def lift(source):
        for k in range(0, chunk, 2):
            bands = []
            for i in (source * chunk + k, source * chunk + k + 1):
                piece = gathered[source, :, pl.ds((k + len(bands)) * nb, nb)]
                bands.append(dot_nt(piece, left_ref[i].reshape(2 * nb, nb)).astype(BF16))
            for member in range(2):
                lifted[source * chunk + k + member, 0] = bands[member][:, :nb]
                lifted[source * chunk + k + member, 1] = bands[member][:, nb:]
            point = source * chunk + k
            above = point // 2
            for slot in range(3):
                p = above - 1 + slot
                picked = [
                    lifted[point + member, jnp.clip(p - row_base(point + member), 0, 1)] for member in range(2)
                ]
                place = jnp.maximum(p, 0)
                matrix = jnp.concatenate([blocks[q, place] for q in range(q_count)], axis=1)
                image = dot_nn(jnp.concatenate(picked, axis=0), matrix).astype(BF16)
                at = p * 6 + 6 + (2 - slot) * 2
                for member in range(2):
                    for q in range(q_count):
                        slots[at + member, q] = image[member * vecs:(member + 1) * vecs, q * nb:(q + 1) * nb]

    lift(col_id)

    def lift_next(step, carry):
        offset = step + 1
        source = lax.rem(col_id // 2 + offset // 2, n_cols // 2) * 2 + lax.rem(core + offset, 2)
        pltpu.make_async_remote_copy(
            src_ref=gathered.at[source], dst_ref=gathered.at[source],
            send_sem=row_send.at[0], recv_sem=row_recv.at[source],
            device_id=(row_id, source), device_id_type=MESH,
        ).wait_recv()
        lift(source)
        return carry

    lax.fori_loop(0, n_cols - 1, lift_next, 0)

    def back_copy(piece, offset):
        peer = row_peer(offset)
        return pltpu.make_async_remote_copy(
            src_ref=back_out.at[piece, peer], dst_ref=back_in.at[piece, row_id],
            send_sem=back_send.at[piece, offset], recv_sem=back_recv.at[piece, row_id],
            device_id=(peer, col_id), device_id_type=MESH,
        )

    pieces = back_out.shape[0]
    span = fine_cols // pieces
    group = 8
    for piece in range(pieces):
        def finish(step, carry):
            j = piece * span + step
            q = col_base(j)
            slot = 1 + q - j // 2

            def add(block, totals):
                first, second = totals
                for k in range(group):
                    i = block * group + k
                    at = spot[i]
                    for dp in range(2):
                        row = (j + 2) * 8 + slot + dp * 3
                        first = first + mix[row, i] * slots[at + 4 * dp, q].astype(F32)
                        second = second + mix[row + 1, i] * slots[at + 4 * dp, q + 1].astype(F32)
                return first, second

            zero = jnp.zeros((vecs, nb), F32)
            first, second = lax.fori_loop(0, fine_rows // group, add, (zero, zero))
            both = jnp.concatenate([first.astype(BF16), second.astype(BF16)], axis=1)
            image = dot_nn(both, right_ref[j].reshape(2 * nb, nb))
            for target in range(n_rows):
                back_out[piece, target, :, pl.ds(pl.multiple_of(step * nb, nb), nb)] = (
                    image[target * share:(target + 1) * share].astype(BF16)
                )
            return carry

        lax.fori_loop(0, span, finish, 0)
        for offset in range(1, n_rows):
            back_copy(piece, offset).start()

    for piece in range(pieces):
        total = back_out[piece, row_id].astype(F32)
        for offset in range(1, n_rows):
            source = row_peer(offset)
            pltpu.make_async_remote_copy(
                src_ref=back_in.at[piece, source], dst_ref=back_in.at[piece, source],
                send_sem=back_send.at[piece, 0], recv_sem=back_recv.at[piece, source],
                device_id=(source, col_id), device_id_type=MESH,
            ).wait_recv()
            total = total + back_in[piece, source].astype(F32)
        adjoint_ref[:, pl.ds(piece * span * nb, span * nb)] = total.astype(BF16)

    for copy in sends:
        copy.wait_send()
    for used, copy in rims:
        pl.when(used)(copy.wait_send)

    @pl.when(core == 1)
    def _():
        def settle(step, carry):
            row, offset = step // (n_cols - 1), step % (n_cols - 1)
            offset = offset + jnp.minimum(offset, 1)
            source = lax.rem(col_id // 2 + offset // 2, n_cols // 2) * 2 + lax.rem(core + offset, 2)
            near_copy(source * held + row).wait_send()
            return carry

        lax.fori_loop(0, held * (n_cols - 1), settle, 0)

    relay.wait_send()
    for step in range(n_cols - 1):
        part_copy(step).wait_send()
        row_copy(step).wait_send()
    for piece in range(pieces):
        for offset in range(1, n_rows):
            back_copy(piece, offset).wait_send()


def body(
    coarse_kernel,
    left_rotation,
    right_rotation,
    fine_map,
    coefficient_index,
    coefficient_table,
    trial_vectors,
):
    n_rows = lax.axis_size("rowk")
    n_cols = lax.axis_size("colk")
    held, coarse_total = coarse_kernel.shape[:2]
    fine_rows = left_rotation.shape[0]
    fine_cols = right_rotation.shape[0]
    nb = left_rotation.shape[2]
    vecs = trial_vectors.shape[0]
    p_count = coarse_total // n_rows + 1
    q_count = coarse_total // n_cols + 1
    chunk = fine_rows // n_cols
    share = vecs // n_rows
    pieces = 4

    sizes = (n_rows, n_cols, held, p_count, q_count, fine_rows, fine_cols, nb, vecs)
    anywhere = pl.BlockSpec(memory_space=pltpu.HBM)
    vmem = pl.BlockSpec(memory_space=pltpu.VMEM)
    smem = pl.BlockSpec(memory_space=pltpu.SMEM)
    dma = pltpu.SemaphoreType.DMA
    return pl.pallas_call(
        functools.partial(operator_kernel, sizes),
        out_shape=(
            jax.ShapeDtypeStruct((vecs, chunk * nb), BF16),
            jax.ShapeDtypeStruct((share, fine_cols * nb), BF16),
        ),
        in_specs=[anywhere, anywhere, anywhere, smem, vmem, smem, anywhere],
        out_specs=(vmem, vmem),
        scratch_shapes=[
            pltpu.VMEM((q_count, p_count, nb, nb), BF16),
            pltpu.VMEM((fine_cols + 6, 3, vecs, nb), F32),
            pltpu.VMEM((fine_rows, 2, q_count, vecs, nb), BF16),
            pltpu.VMEM((p_count * 6, vecs, nb), BF16),
            pltpu.VMEM((n_cols, vecs, chunk * nb), BF16),
            pltpu.VMEM((n_cols, vecs, chunk * nb), BF16),
            pltpu.VMEM((n_cols, vecs, chunk * nb), BF16),
            pltpu.VMEM((fine_rows, 2, vecs, nb), BF16),
            pltpu.VMEM((p_count * 6 + 6, q_count, vecs, nb), BF16),
            pltpu.VMEM((pieces, n_rows, share, fine_cols * nb // pieces), BF16),
            pltpu.VMEM((pieces, n_rows, share, fine_cols * nb // pieces), BF16),
            pltpu.VMEM(left_rotation.shape, BF16),
            pltpu.VMEM(right_rotation.shape, BF16),
            pltpu.VMEM(trial_vectors.shape, BF16),
            pltpu.VMEM(((fine_cols + 6) * 8, 128), F32),
            pltpu.SMEM(((fine_cols + 6) * 8, 128), F32),
            pltpu.SMEM((fine_rows,), jnp.int32),
            dma((held, 2)),
            dma((3,)),
            dma(()),
            dma((held * n_cols,)),
            dma((p_count,)),
            dma((held * n_cols,)),
            dma((p_count,)),
            dma((p_count,)),
            dma(()),
            dma(()),
            dma((n_cols,)),
            dma((n_cols,)),
            dma((n_cols,)),
            dma((n_cols,)),
            dma((pieces, n_rows)),
            dma((pieces, n_rows)),
        ],
        compiler_params=pltpu.CompilerParams(
            collective_id=0, has_side_effects=True, vmem_limit_bytes=52 * 1024 * 1024
        ),
        name="operator_images",
    )(
        coarse_kernel, left_rotation, right_rotation, fine_map, coefficient_index.transpose(1, 2, 0),
        coefficient_table, trial_vectors
    )


def solution(mesh):
    return jax.shard_map(
        body,
        mesh=mesh,
        in_specs=(
            P(("rowk", "colk"), None, None, None),
            P("rowk", None, None, None),
            P("colk", None, None, None),
            P(),
            P("rowk", "colk", None),
            P(),
            P(None, "colk"),
        ),
        out_specs=(P(None, ("rowk", "colk")), P("rowk", "colk")),
        check_vma=False,
    )
```
